32 devices in a mesh: dp: 16 (over z, x, core), tensor: 2 (over y).
Axes of the slice: x: 2, y: 2, z: 4, core: 2. Of those that a mesh axis runs over, the one named last changes fastest.
Arguments:
- tokens: bfloat16 [512, 64, 768], P('tensor', 'dp'), may hold values from -6 to 6
- lengths: int32 [64], P('dp'), may hold values from 64 to 512, as said below
- w_qkv: bfloat16 [3, 768, 768], P(None, 'dp', 'tensor'), may hold values from -0.21875 to 0.21875
- qkv_bias: bfloat16 [2, 768], P(None, ('tensor', 'dp')), may hold values from -3 to 3
- w_out: bfloat16 [768, 768], P('tensor', 'dp'), may hold values from -0.875 to 0.875
- w_in: bfloat16 [768, 3072], P('dp', 'tensor'), may hold values from -0.21875 to 0.21875
- b_in: bfloat16 [3072], P(('tensor', 'dp')), may hold values from -3 to 3
- w_down: bfloat16 [3072, 768], P('tensor', 'dp'), may hold values from -0.109375 to 0.109375
- norm_gains: bfloat16 [2, 768], P(None, ('tensor', 'dp')), may hold values from 0.5 to 1.5
- row_biases: bfloat16 [4, 768], P(None, ('tensor', 'dp')), may hold values from -2 to 2
- cotangent: bfloat16 [512, 64, 768], P('tensor', 'dp'), may hold values from -6 to 6
Outputs:
- out: bfloat16 [512, 64, 768], P('tensor', 'dp')
- d_tokens: float32 [512, 64, 768], P('tensor', 'dp')
- grad_qkv: float32 [3, 768, 768], P(None, 'dp', 'tensor')
- grad_qkv_bias: float32 [2, 768], P(None, ('tensor', 'dp'))
- grad_out: float32 [768, 768], P('tensor', 'dp')
- grad_in: float32 [768, 3072], P('dp', 'tensor')
- grad_in_bias: float32 [3072], P(('tensor', 'dp'))
- grad_down: float32 [3072, 768], P('tensor', 'dp')
- grad_gains: float32 [2, 768], P(None, ('tensor', 'dp'))
- grad_biases: float32 [4, 768], P(None, ('tensor', 'dp'))
The draws below stay inside these ranges and needn't reach their ends.
Inputs may be any that keep to these rules, and one draw needn't show every extreme that they name: `lengths`: each aligned run of 4 sequences holds at least one sequence of length 512; which one is drawn.
All inputs are finite; a program needn't handle non-finite values.
Results may differ from the reference program's by a relative error of at most 0.017.
Values may be sent and summed in bfloat16 or wider, within the bound.
No kernel may reach another device: no remote copies, remote signals or barrier semaphores. Data moves between devices by JAX's collectives and lax.ppermute only.
A program may use at most 192 MiB of HBM per device.

```python
import math
import jax
import jax.numpy as jnp
from jax import lax

D = 768
HEADS = 12
HEAD_DIM = 64
FF = 3072
SEQ_LEN = 512
SEQ_DEV = 4
SEQS = 64


def draw_lengths(key, part):
    key = jax.random.fold_in(key, 7)
    first_key, second_key = jax.random.split(key)
    shortest = max(1, SEQ_LEN // 8)
    drawn = jax.random.randint(first_key, (SEQS,), shortest, SEQ_LEN + 1, dtype=jnp.int32)
    chosen = jax.random.randint(second_key, (SEQS // SEQ_DEV,), 0, SEQ_DEV, dtype=jnp.int32)
    slots = jnp.arange(SEQS, dtype=jnp.int32) % SEQ_DEV
    group_choice = jnp.repeat(chosen, SEQ_DEV)
    return jnp.where(slots == group_choice, SEQ_LEN, drawn).astype(jnp.int32)


def levels(rng, shape, pieces, least, high):
    factor_of = 1.0
    for axis_at, parts in pieces:
        heights = jax.random.uniform(jax.random.fold_in(jax.random.fold_in(rng, 6), axis_at), (parts,), jnp.float32, least / len(pieces), high / len(pieces))
        factor_of = factor_of * jnp.repeat(jnp.exp(heights), shape[axis_at] // parts).reshape((-1,) + (1,) * (len(shape) - 1 - axis_at))
    return factor_of


def normal_values(key, shape, deviation, limit, cuts=(), kind=jnp.bfloat16):
    values = deviation * jax.random.normal(key, shape, jnp.float32)
    if cuts:
        values = values * levels(key, shape, cuts, -0.22, 0.18)
    return jnp.clip(values, -limit, limit).astype(kind)


def setup_inputs(seed: int = 0) -> dict:
    seeds = jax.random.split(jax.random.key(seed), 12)
    return {
        "tokens": normal_values(seeds[0], (SEQ_LEN, SEQS, D), 1.0, 6.0, ((0, 2), (1, 16))),
        "lengths": draw_lengths(jax.random.fold_in(seeds[11], 71), 0),
        "w_qkv": normal_values(seeds[2], (3, D, D), D ** -0.5, 0.21875, ((1, 16), (2, 2))),
        "qkv_bias": normal_values(seeds[3], (2, D), 0.5, 3.0, ((1, 32),)),
        "w_out": normal_values(seeds[4], (D, D), (D // 16) ** -0.5, 0.875, ((0, 2), (1, 16))),
        "w_in": normal_values(seeds[5], (D, FF), D ** -0.5, 0.21875, ((0, 16), (1, 2))),
        "b_in": normal_values(seeds[6], (FF,), 0.5, 3.0, ((0, 32),)),
        "w_down": normal_values(seeds[7], (FF, D), FF ** -0.5, 0.109375, ((0, 2), (1, 16))),
        "norm_gains": jnp.clip(1.0 + 0.1 * jax.random.normal(seeds[8], (2, D), jnp.float32), 0.5, 1.5).astype(jnp.bfloat16),
        "row_biases": normal_values(seeds[9], (4, D), 0.3, 2.0, ((1, 32),)),
        "cotangent": normal_values(seeds[10], (SEQ_LEN, SEQS, D), 1.0, 6.0, ((0, 2), (1, 16))),
    }


precise = lax.Precision.HIGHEST
norm_eps = 1e-12

@jax.custom_vjp
def low(v):
    return lax.optimization_barrier(v.astype(jnp.bfloat16)).astype(jnp.float32)

@jax.custom_vjp
def low_back(v):
    return v

def low_keep(v):
    return (low(v), None)

def low_pass(kept, grad):
    return (grad,)

def back_keep(v):
    return (v, None)

def back_low(kept, grad):
    return (low(grad),)
low.defvjp(low_keep, low_pass)
low_back.defvjp(back_keep, back_low)

def layer_norm(values, gain, shift):
    centered = values - lax.optimization_barrier(jnp.mean(values, axis=-1, keepdims=True))
    inverse = lax.rsqrt(lax.optimization_barrier(jnp.mean(centered * centered, axis=-1, keepdims=True)) + norm_eps)
    return centered * inverse * gain + shift

def block_layer(inputs, weights, seq_lengths):
    w_qkv, qkv_bias, w_out, w_in, b_in, w_down, norm_gains, row_biases = weights
    seq_len, count, width = inputs.shape
    rows = inputs.reshape(seq_len * count, width)
    query = low_back(low(jnp.dot(rows, w_qkv[0], precision=precise) + qkv_bias[0]))
    keys = low_back(low(jnp.dot(rows, w_qkv[1], precision=precise)))
    values = low_back(low(jnp.dot(rows, w_qkv[2], precision=precise) + qkv_bias[1]))
    head_shape = (seq_len, count, HEADS, HEAD_DIM)
    scale_factor = 1.0 / math.sqrt(HEAD_DIM)
    scores = jnp.einsum('lbhe,mbhe->bhlm', query.reshape(head_shape), keys.reshape(head_shape), precision=precise) * scale_factor
    positions = jnp.arange(seq_len, dtype=jnp.int32)
    valid = positions[None, :] < seq_lengths[:, None]
    scores = jnp.where(valid[:, None, None, :], scores, -1000000000.0)
    scores = low_back(scores)
    probs = jax.nn.softmax(scores, axis=-1)
    context = jnp.einsum('bhlm,mbhe->lbhe', low(probs), values.reshape(head_shape), precision=precise)
    context = low_back(low(context.reshape(seq_len * count, width)))
    attended = low_back(jnp.dot(context, w_out, precision=precise))
    first = layer_norm(rows + attended + row_biases[0], norm_gains[0], row_biases[1])
    before = low_back(jnp.dot(low(first), w_in, precision=precise) + b_in)
    hidden = low(jax.nn.gelu(before, approximate=False))
    mixed = low_back(jnp.dot(hidden, w_down, precision=precise))
    output = layer_norm(first + mixed + row_biases[2], norm_gains[1], row_biases[3])
    return output.reshape(seq_len, count, width)

def reference(tokens, lengths, w_qkv, qkv_bias, w_out, w_in, b_in, w_down, norm_gains, row_biases, cotangent):
    params = tuple((weight.astype(jnp.float32) for weight in (w_qkv, qkv_bias, w_out, w_in, b_in, w_down, norm_gains, row_biases)))
    group = math.gcd(SEQS, max(1, 4096 // SEQ_LEN))
    block_count = SEQS // group

    def one_block(totals, index):
        start = (index * group).astype(jnp.int32)
        inputs = lax.dynamic_slice_in_dim(tokens, start, group, 1).astype(jnp.float32)
        grad_output = lax.dynamic_slice_in_dim(cotangent, start, group, 1).astype(jnp.float32)
        seq_lengths = lax.dynamic_slice_in_dim(lengths, start, group, 0)

        def forward(values, weights):
            return block_layer(values, weights, seq_lengths)
        result, pullback = jax.vjp(forward, inputs, params)
        grad_inputs, grad_params = pullback(grad_output)
        totals = jax.tree.map(lambda total, extra: total + extra, totals, grad_params)
        return (totals, (result.astype(jnp.bfloat16), grad_inputs))
    zeros = tuple((jnp.zeros(weight.shape, jnp.float32) for weight in params))
    totals, stacked = lax.scan(one_block, zeros, jnp.arange(block_count, dtype=jnp.int32))
    outputs = jnp.transpose(stacked[0], (1, 0, 2, 3)).reshape(SEQ_LEN, SEQS, D)
    grad_tokens = jnp.transpose(stacked[1], (1, 0, 2, 3)).reshape(SEQ_LEN, SEQS, D)
    return (outputs, grad_tokens, totals[0], totals[1], totals[2], totals[3], totals[4], totals[5], totals[6], totals[7])
```

```python
import functools

import jax
import jax.numpy as jnp
from jax import lax
from jax.experimental import pallas as pl
from jax.experimental.pallas import tpu as pltpu
from jax.sharding import PartitionSpec as P

HEAD_DIM = 64
BOTH = ("dp", "tensor")
BIT_Y, BIT_CORE, BIT_X, BIT_Z = 1, 2, 4, 8
PLACES = 32

norm_eps = 1e-12
bf16 = jnp.bfloat16
f32 = jnp.float32


def norm_forward(values, gain, shift):
    centered = values - jnp.mean(values, axis=-1, keepdims=True)
    inverse = lax.rsqrt(jnp.mean(centered * centered, axis=-1, keepdims=True) + norm_eps)
    normed = centered * inverse
    return (normed * gain + shift, normed, inverse)


def norm_backward(grad, normed, inverse, gain):
    scaled = grad * gain
    inner = (
        scaled
        - jnp.mean(scaled, axis=-1, keepdims=True)
        - normed * jnp.mean(scaled * normed, axis=-1, keepdims=True)
    )
    return inner * inverse


def dot(left, right):
    return jnp.dot(left, right, preferred_element_type=f32)


def dot_nt(left, right):
    return lax.dot_general(left, right, (((1,), (1,)), ((), ())), preferred_element_type=f32)


def dot_tn(left, right):
    return lax.dot_general(left, right, (((0,), (0,)), ((), ())), preferred_element_type=f32)


def three_parts(value):
    high = value.astype(bf16)
    rest = value - high.astype(f32)
    middle = rest.astype(bf16)
    low = (rest - middle.astype(f32)).astype(bf16)
    return high.astype(f32), middle.astype(f32), low.astype(f32)


def key_bias(length, own, count):
    place = lax.broadcasted_iota(jnp.int32, (count, 128), 0)
    place = (place + own * (count // 2)) & (count - 1)
    return jnp.where(place < length, 0.0, -1000000000.0)


def attend_kernel(info_ref, q_ref, k_ref, v_ref, ctx_ref, lse_ref):
    count = q_ref.shape[0]
    lane = lax.broadcasted_iota(jnp.int32, (count, 128), 1)
    bias = key_bias(info_ref[1 + pl.program_id(0)], info_ref[0], count)
    query = q_ref[...].astype(f32) * (HEAD_DIM**-0.5)
    keys = k_ref[...].astype(f32)
    values = v_ref[...].astype(f32)
    contexts, sums = [], []
    for head in range(2):
        mine = (lane < 64) if head == 0 else (lane >= 64)
        extra = 64 * (1 - head)
        query_h = jnp.where(mine, query, jnp.where(lane == extra, 1.0, 0.0)).astype(bf16)
        keys_h = jnp.where(mine, keys, jnp.where(lane == extra, bias, 0.0)).astype(bf16)
        values_h = jnp.where(mine, values, 1.0).astype(bf16)
        scores = dot_nt(query_h, keys_h)
        peak = jnp.max(scores, axis=1, keepdims=True)
        exponent = jnp.exp(scores - peak).astype(bf16)
        mixed = dot(exponent, values_h)
        total = pltpu.roll(mixed, 64, 1)
        contexts.append(mixed / total)
        sums.append(peak + jnp.log(mixed))
    low = lane < 64
    ctx_ref[...] = jnp.where(low, contexts[0], contexts[1]).astype(bf16)
    lse_ref[...] = jnp.where(low, sums[1], sums[0])


def attend(info, qkv, seqs):
    rows, triple = qkv.shape
    count, pairs = rows // seqs, triple // 3 // 128
    block = lambda at: pl.BlockSpec((count, 128), lambda s, p, info: (s, p + at * pairs))
    return pl.pallas_call(
        attend_kernel,
        grid_spec=pltpu.PrefetchScalarGridSpec(
            num_scalar_prefetch=1,
            grid=(seqs, pairs),
            in_specs=[block(0), block(1), block(2)],
            out_specs=[block(0), block(0)],
        ),
        out_shape=[
            jax.ShapeDtypeStruct((rows, triple // 3), bf16),
            jax.ShapeDtypeStruct((rows, triple // 3), f32),
        ],
        compiler_params=pltpu.CompilerParams(vmem_limit_bytes=48 << 20),
        name="attend",
    )(info, qkv, qkv, qkv)


def attend_back_kernel(
    info_ref, q_ref, k_ref, v_ref, ctx_ref, lse_ref, dctx_ref, dq_ref, dk_ref, dv_ref
):
    count = q_ref.shape[0]
    lane = lax.broadcasted_iota(jnp.int32, (count, 128), 1)
    bias = key_bias(info_ref[1 + pl.program_id(0)], info_ref[0], count)
    scale = HEAD_DIM**-0.5
    query = q_ref[...].astype(f32) * scale
    query_low = query.astype(bf16)
    keys_low = k_ref[...]
    keys = keys_low.astype(f32)
    values = v_ref[...].astype(f32)
    grad_low = dctx_ref[...]
    grad = grad_low.astype(f32)
    product = grad * ctx_ref[...].astype(f32)
    lse_parts = three_parts(-lse_ref[...])
    outs = []
    for head in range(2):
        mine = (lane < 64) if head == 0 else (lane >= 64)
        at = lane - 64 * (1 - head)
        ones = jnp.where((at >= 1) & (at <= 3), 1.0, 0.0)

        def spread(parts, first):
            high, middle, low = parts
            value = jnp.where(at == 2, middle, jnp.where(at == 3, low, 0.0))
            return jnp.where(at == 1, high, jnp.where(at == 0, first, value))

        query_h = jnp.where(mine, query, spread(lse_parts, 1.0)).astype(bf16)
        keys_h = jnp.where(mine, keys, jnp.where(at == 0, bias, ones)).astype(bf16)
        inner = -jnp.sum(jnp.where(mine, product, 0.0), axis=1, keepdims=True)
        inner = jnp.broadcast_to(inner, (count, 128))
        grad_h = jnp.where(mine, grad, spread(three_parts(inner), 0.0)).astype(bf16)
        values_h = jnp.where(mine, values, ones).astype(bf16)
        probs = jnp.exp(dot_nt(keys_h, query_h))
        grad_probs = dot_nt(values_h, grad_h)
        grad_scores = (probs * grad_probs).astype(bf16)
        grad_values = dot(probs.astype(bf16), grad_low)
        grad_keys = dot(grad_scores, query_low)
        grad_query = dot_tn(grad_scores, keys_low) * scale
        outs.append((grad_query, grad_keys, grad_values))
    low = lane < 64
    for ref, first, second in zip((dq_ref, dk_ref, dv_ref), outs[0], outs[1]):
        ref[...] = jnp.where(low, first, second).astype(bf16)


def attend_back(info, qkv, ctx, lse, grad_ctx, seqs):
    rows, triple = qkv.shape
    count, pairs = rows // seqs, triple // 3 // 128
    block = lambda at: pl.BlockSpec((count, 128), lambda s, p, info: (s, p + at * pairs))
    return pl.pallas_call(
        attend_back_kernel,
        grid_spec=pltpu.PrefetchScalarGridSpec(
            num_scalar_prefetch=1,
            grid=(seqs, pairs),
            in_specs=[block(0), block(1), block(2), block(0), block(0), block(0)],
            out_specs=[block(0)] * 3,
        ),
        out_shape=[jax.ShapeDtypeStruct((rows, triple // 3), bf16)] * 3,
        compiler_params=pltpu.CompilerParams(vmem_limit_bytes=48 << 20),
        name="attend_back",
    )(info, qkv, qkv, qkv, ctx, lse, grad_ctx)


def gelu_and_slope(value):
    size = jnp.abs(value)
    near = 1.0 / (1.0 + (0.3275911 * 0.7071067811865476) * size)
    bell = jnp.exp(-0.5 * (value * value))
    poly = 0.5 * 1.061405429
    poly = poly * near + 0.5 * -1.453152027
    poly = poly * near + 0.5 * 1.421413741
    poly = poly * near + 0.5 * -0.284496736
    poly = poly * near + 0.5 * 0.254829592
    tail = poly * near * bell
    phi = jnp.where(value >= 0, 1.0 - tail, tail)
    return value * phi, phi + value * (bell * 0.3989422804014327)


def up_kernel(h_ref, w_ref, b_ref, g_ref, s_ref):
    rows = h_ref.shape[0]
    step = 256
    for at in range(0, rows, step):
        part = pl.ds(at, step)
        before = dot(h_ref[part, :], w_ref[...]) + b_ref[...]
        hidden, slope = gelu_and_slope(before)
        g_ref[part, :] = hidden.astype(bf16)
        s_ref[part, :] = slope.astype(bf16)


def up(first_low, w_in, b_in):
    rows, width = first_low.shape
    units = w_in.shape[1]
    step = 512
    return pl.pallas_call(
        up_kernel,
        grid=(units // step,),
        in_specs=[
            pl.BlockSpec((rows, width), lambda i: (0, 0)),
            pl.BlockSpec((width, step), lambda i: (0, i)),
            pl.BlockSpec((1, step), lambda i: (0, i)),
        ],
        out_specs=[pl.BlockSpec((rows, step), lambda i: (0, i))] * 2,
        out_shape=[jax.ShapeDtypeStruct((rows, units), bf16)] * 2,
        compiler_params=pltpu.CompilerParams(vmem_limit_bytes=48 << 20),
        name="up",
    )(first_low, w_in, b_in)


def swap(value, even, odd):
    pairs = [(i, i ^ (odd if i & BIT_CORE else even)) for i in range(PLACES)]
    return lax.ppermute(value, BOTH, pairs)


def gather_parts(shard):
    group = jnp.stack([shard] + [swap(shard, BIT_Z * k, BIT_Z * k) for k in (1, 2, 3)])
    near = swap(group, BIT_X, BIT_Y)
    far = swap(group, BIT_Y, BIT_X)
    corner = swap(near, BIT_Y, BIT_X)
    own = [group, near, far, corner]
    return own + [swap(part, BIT_CORE, BIT_CORE) for part in own]


def scatter_parts(mine, theirs):
    total = mine.astype(f32) + swap(theirs, BIT_CORE, BIT_CORE).astype(f32)
    far = swap(total[2].astype(bf16), BIT_Y, BIT_X).astype(f32)
    corner = swap(total[3].astype(bf16), BIT_Y, BIT_X).astype(f32)
    near = swap((total[1] + corner).astype(bf16), BIT_X, BIT_Y).astype(f32)
    group = total[0] + far + near
    result = group[0]
    for k in (1, 2, 3):
        result = result + swap(group[k].astype(bf16), BIT_Z * k, BIT_Z * k).astype(f32)
    return result


def slots(me):
    core = (me >> 1) & 1
    for other in (0, 1):
        along = jnp.where((core ^ other) == 0, BIT_X, BIT_Y)
        across = (BIT_X + BIT_Y) - along
        for part, bits in enumerate((0, along, across, BIT_X + BIT_Y)):
            for k in range(4):
                yield other, part, k, me ^ (other * BIT_CORE) ^ bits ^ (k * BIT_Z)


def window(ref, move, place):
    _, rows, columns, _, step, start, wide = move
    row = pl.multiple_of((place >> 1 if wide else place) * step, 16)
    if not wide:
        return ref.at[pl.ds(row, rows), :]
    column = pl.multiple_of(start + (place & 1) * columns, 128)
    return ref.at[pl.ds(row, rows), pl.ds(column, columns)]


def place_kernel(me_ref, *refs, moves, outs):
    ins, wholes, sems = refs[:8], refs[8 : 8 + outs], refs[8 + outs]
    for other, part, k, place in slots(me_ref[0]):
        for move in moves:
            source, rows, to = move[0], move[1], move[3]
            pltpu.make_async_copy(
                ins[4 * other + part].at[k, pl.ds(source, rows), :],
                window(wholes[to], move, place),
                sems.at[to],
            ).start()
    for to in range(outs):
        pltpu.make_async_copy(wholes[to], wholes[to], sems.at[to]).wait()


def spread_kernel(me_ref, *refs, moves, ins):
    wholes, halves, sems = refs[:ins], refs[ins : ins + 2], refs[ins + 2]
    for other, part, k, place in slots(me_ref[0]):
        for move in moves:
            source, rows, to = move[0], move[1], move[3]
            pltpu.make_async_copy(
                window(wholes[to], move, place),
                halves[other].at[part, k, pl.ds(source, rows), :],
                sems.at[other],
            ).start()
    for other in (0, 1):
        pltpu.make_async_copy(halves[other], halves[other], sems.at[other]).wait()


anywhere = pl.BlockSpec(memory_space=pl.ANY)
on_core = pl.BlockSpec(memory_space=pltpu.VMEM)


def place(me, parts, moves, shapes):
    return pl.pallas_call(
        functools.partial(place_kernel, moves=moves, outs=len(shapes)),
        in_specs=[pl.BlockSpec(memory_space=pltpu.SMEM)] + [anywhere] * 8,
        out_specs=[on_core] * len(shapes),
        out_shape=[jax.ShapeDtypeStruct(shape, bf16) for shape in shapes],
        compiler_params=pltpu.CompilerParams(vmem_limit_bytes=48 << 20),
        scratch_shapes=[pltpu.SemaphoreType.DMA((len(shapes),))],
        name="place",
    )(me, *parts)


def spread(me, wholes, moves, rows, columns):
    return pl.pallas_call(
        functools.partial(spread_kernel, moves=moves, ins=len(wholes)),
        in_specs=[pl.BlockSpec(memory_space=pltpu.SMEM)] + [anywhere] * len(wholes),
        out_specs=[on_core] * 2,
        out_shape=[jax.ShapeDtypeStruct((4, 4, rows, columns), bf16)] * 2,
        compiler_params=pltpu.CompilerParams(vmem_limit_bytes=48 << 20),
        scratch_shapes=[pltpu.SemaphoreType.DMA((2,))],
        name="spread",
    )(me, *wholes)


def move_list(row, blocks, vectors):
    moves, at = [], 0
    for to, columns, starts in blocks:
        for start in starts:
            moves.append((at, row, columns, to, row, start, True))
            at += row
    if vectors:
        moves.append((at, 16, blocks[0][1], vectors, 16, 0, False))
    return tuple(moves)


def gather_whole(me, shard, moves, shapes, direct):
    if direct:
        return place(me, gather_parts(shard), moves, shapes)
    everything = lax.all_gather(shard, BOTH, axis=0)
    places = everything.shape[0]
    wholes = [jnp.zeros((0,), bf16)] * len(shapes)
    for to, shape in enumerate(shapes):
        pieces = []
        for source, rows, columns, at, _, _, wide in moves:
            if at != to:
                continue
            piece = everything[:, source : source + rows]
            if wide:
                piece = piece.reshape(places // 2, 2, rows, columns).transpose(0, 2, 1, 3)
                pieces.append(piece.reshape(places // 2 * rows, 2 * columns))
            else:
                pieces.append(piece.reshape(shape))
        wholes[to] = jnp.concatenate(pieces, axis=1)
    return wholes


def scatter_whole(me, wholes, moves, rows, columns, direct):
    if direct:
        return scatter_parts(*spread(me, wholes, moves, rows, columns))
    pieces = []
    for _, count, wide_columns, to, step, start, wide in moves:
        whole = wholes[to]
        if wide:
            whole = whole[:, start : start + 2 * wide_columns]
            whole = whole.reshape(-1, count, 2, wide_columns).transpose(0, 2, 1, 3)
        pieces.append(whole.reshape(-1, count, wide_columns))
    return lax.psum_scatter(
        jnp.concatenate(pieces, axis=1), BOTH, scatter_dimension=0, tiled=True
    )[0].astype(f32)


def shards(
    tokens, lengths, w_qkv, qkv_bias, w_out, w_in, b_in, w_down, norm_gains, row_biases, cotangent, direct
):
    half_len, seq_count, width = tokens.shape
    own = lax.axis_index("tensor")
    me = (lax.axis_index("dp") * 2 + own).astype(jnp.int32).reshape(1)
    seqs = seq_count // 2
    row = w_qkv.shape[1]
    local_width, local_units = w_qkv.shape[2], w_in.shape[1]
    count = qkv_bias.shape[1]
    units = 2 * local_units
    places = width // row * 2
    total_rows = seqs * 2 * half_len

    def trade(value):
        return lax.ppermute(value, "tensor", [(0, 1), (1, 0)])

    def to_rows(value):
        by_seq = jnp.swapaxes(value, 0, 1)
        kept = lax.dynamic_slice_in_dim(by_seq, own * seqs, seqs, 0)
        sent = lax.dynamic_slice_in_dim(by_seq, (1 - own) * seqs, seqs, 0)
        return jnp.stack([kept, trade(sent)], axis=1).reshape(total_rows, width)

    def from_rows(value, kind):
        halves = value.reshape(seqs, 2, half_len, width)
        kept = halves[:, 0]
        got = trade(halves[:, 1].astype(bf16)).astype(value.dtype)
        first = jnp.where(own == 0, kept, got)
        second = jnp.where(own == 0, got, kept)
        return jnp.swapaxes(jnp.concatenate([first, second], axis=0), 0, 1).astype(kind)

    def pack(pieces, kind):
        flat = jnp.concatenate([piece.reshape(piece.shape[0], -1) for piece in pieces], axis=1)
        flat = jnp.pad(flat, ((0, 0), (0, local_width - flat.shape[1])))
        return jnp.pad(flat[:, None, :], ((0, 0), (0, 15), (0, 0))).astype(kind)

    rows = to_rows(tokens)
    vectors = pack(
        [qkv_bias[None], b_in[None], norm_gains[None], row_biases[None]], bf16
    ).reshape(16, local_width)
    attn_shard = jnp.concatenate([w_qkv.reshape(3 * row, local_width), w_out.T, vectors], axis=0)
    qkv_starts = (0, width, 2 * width)
    attn_moves = move_list(row, [(0, local_width, qkv_starts), (1, local_width, (0,))], 2)
    wq, wo, vector_rows = gather_whole(
        me,
        attn_shard,
        attn_moves,
        [(width, 3 * width), (width, width), (places * 16, local_width)],
        direct,
    )
    mlp_moves = move_list(row, [(0, local_units, (0,))], None)
    (wi,) = gather_whole(me, w_in, mlp_moves, [(width, units)], direct)
    (wd,) = gather_whole(me, w_down.T, mlp_moves, [(width, units)], direct)

    flat = vector_rows.reshape(places // 2, 2, 16, local_width)[:, :, 0]
    flat = jnp.swapaxes(flat, 0, 1).reshape(places, local_width)

    def vector(at, lines, size):
        piece = flat[:, at : at + lines * size].reshape(places, lines, size)
        return jnp.swapaxes(piece, 0, 1).reshape(lines, places * size)

    wide = b_in.shape[0]
    bias_pair = vector(0, 2, count)
    b_in_all = vector(2 * count, 1, wide)
    gains = vector(2 * count + wide, 2, count).astype(f32)
    shifts = vector(4 * count + wide, 4, count).astype(f32)

    mine_lengths = lax.dynamic_slice_in_dim(lengths, own * seqs, seqs, 0)
    info = jnp.concatenate([own.reshape(1).astype(jnp.int32), mine_lengths])

    qkv_shift = jnp.concatenate([bias_pair[0], jnp.zeros((width,), bf16), bias_pair[1]])
    qkv = (dot(rows, wq) + qkv_shift.astype(f32)).astype(bf16)
    ctx, lse = attend(info, qkv, seqs)
    attended = dot_nt(ctx, wo)
    first, normed_one, inverse_one = norm_forward(
        rows.astype(f32) + attended + shifts[0], gains[0], shifts[1]
    )
    first_low = first.astype(bf16)
    hidden, slope = up(first_low, wi, b_in_all.astype(f32))
    mixed = dot_nt(hidden, wd)
    output, normed_two, inverse_two = norm_forward(first + mixed + shifts[2], gains[1], shifts[3])
    out = from_rows(output.astype(bf16), bf16)

    grad_output = to_rows(cotangent).astype(f32)
    grad_gain_two = jnp.sum(grad_output * normed_two, axis=0)
    grad_shift_two = jnp.sum(grad_output, axis=0)
    grad_second = norm_backward(grad_output, normed_two, inverse_two, gains[1])
    grad_down_bias = jnp.sum(grad_second, axis=0)
    mixed_grad = grad_second.astype(bf16)
    grad_wd = dot_tn(mixed_grad, hidden).astype(bf16)
    grad_down = scatter_whole(me, [grad_wd], mlp_moves, row, local_units, direct).T
    grad_before = (dot(mixed_grad, wd) * slope.astype(f32)).astype(bf16)
    grad_in_bias = jnp.sum(grad_before, axis=0, dtype=f32)
    grad_wi = dot_tn(first_low, grad_before).astype(bf16)
    grad_in = scatter_whole(me, [grad_wi], mlp_moves, row, local_units, direct)
    grad_first = dot_nt(grad_before, wi) + grad_second
    grad_gain_one = jnp.sum(grad_first * normed_one, axis=0)
    grad_shift_one = jnp.sum(grad_first, axis=0)
    grad_resid = norm_backward(grad_first, normed_one, inverse_one, gains[0])
    grad_out_bias = jnp.sum(grad_resid, axis=0)
    attn_grad = grad_resid.astype(bf16)
    grad_wo = dot_tn(attn_grad, ctx).astype(bf16)
    out_moves = move_list(row, [(0, local_width, (0,))], None)
    grad_out = scatter_whole(me, [grad_wo], out_moves, row, local_width, direct).T
    grad_ctx = dot(attn_grad, wo).astype(bf16)
    grad_query, grad_keys, grad_values = attend_back(info, qkv, ctx, lse, grad_ctx, seqs)
    grad_triple = jnp.concatenate([grad_query, grad_keys, grad_values], axis=1)
    grad_wq = dot_tn(rows, grad_triple).astype(bf16)

    def shares(value, lines):
        size = value.size // lines // places
        piece = value.reshape(lines, 2, places // 2, size)
        return piece.transpose(2, 1, 0, 3).reshape(places, lines * size)

    grad_pair = jnp.stack(
        [jnp.sum(grad_query, axis=0, dtype=f32), jnp.sum(grad_values, axis=0, dtype=f32)]
    )
    grad_vectors = pack(
        [
            shares(grad_pair, 2),
            shares(grad_in_bias, 1),
            shares(jnp.stack([grad_gain_one, grad_gain_two]), 2),
            shares(
                jnp.stack([grad_out_bias, grad_shift_one, grad_down_bias, grad_shift_two]), 4
            ),
        ],
        bf16,
    ).reshape(places * 16, local_width)
    qkv_moves = move_list(row, [(0, local_width, qkv_starts)], 1)
    attn_piece = scatter_whole(
        me, [grad_wq, grad_vectors], qkv_moves, 3 * row + 16, local_width, direct
    )
    grad_qkv = attn_piece[: 3 * row].reshape(3, row, local_width)
    line = attn_piece[3 * row]
    grad_tokens = dot_nt(grad_triple, wq) + grad_resid
    d_tokens = from_rows(grad_tokens, f32)

    def cut(at, lines, size):
        return line[at : at + lines * size].reshape(lines, size)

    return (
        out,
        d_tokens,
        grad_qkv,
        cut(0, 2, count),
        grad_out,
        grad_in,
        cut(2 * count, 1, wide)[0],
        grad_down,
        cut(2 * count + wide, 2, count),
        cut(4 * count + wide, 4, count),
    )


def solution(mesh):
    placed = (
        P("tensor", "dp", None),
        P("dp"),
        P(None, "dp", "tensor"),
        P(None, ("tensor", "dp")),
        P("tensor", "dp"),
        P("dp", "tensor"),
        P(("tensor", "dp")),
        P("tensor", "dp"),
        P(None, ("tensor", "dp")),
        P(None, ("tensor", "dp")),
        P("tensor", "dp", None),
    )
    direct = mesh.shape["tensor"] == 2 and mesh.shape["dp"] * 2 == PLACES
    return jax.shard_map(
        functools.partial(shards, direct=direct),
        mesh=mesh,
        in_specs=placed,
        out_specs=(
            P("tensor", "dp", None),
            P("tensor", "dp", None),
            P(None, "dp", "tensor"),
            P(None, ("tensor", "dp")),
            P("tensor", "dp"),
            P("dp", "tensor"),
            P(("tensor", "dp")),
            P("tensor", "dp"),
            P(None, ("tensor", "dp")),
            P(None, ("tensor", "dp")),
        ),
        check_vma=False,
    )
```

```python
import functools

import jax
import jax.numpy as jnp
from jax import lax
from jax.experimental import pallas as pl
from jax.experimental.pallas import tpu as pltpu
from jax.sharding import PartitionSpec as P

HEAD_DIM = 64
BOTH = ("dp", "tensor")
BIT_Y, BIT_CORE, BIT_X, BIT_Z = 1, 2, 4, 8
PLACES = 32

norm_eps = 1e-12
bf16 = jnp.bfloat16
f32 = jnp.float32


def norm_forward(values, gain, shift):
    centered = values - jnp.mean(values, axis=-1, keepdims=True)
    inverse = lax.rsqrt(jnp.mean(centered * centered, axis=-1, keepdims=True) + norm_eps)
    normed = centered * inverse
    return (normed * gain + shift, normed, inverse)


def norm_backward(grad, normed, inverse, gain):
    scaled = grad * gain
    inner = (
        scaled
        - jnp.mean(scaled, axis=-1, keepdims=True)
        - normed * jnp.mean(scaled * normed, axis=-1, keepdims=True)
    )
    return inner * inverse


def dot(left, right):
    return jnp.dot(left, right, preferred_element_type=f32)


def dot_nt(left, right):
    return lax.dot_general(left, right, (((1,), (1,)), ((), ())), preferred_element_type=f32)


def dot_tn(left, right):
    return lax.dot_general(left, right, (((0,), (0,)), ((), ())), preferred_element_type=f32)


def three_parts(value):
    high = value.astype(bf16)
    rest = value - high.astype(f32)
    middle = rest.astype(bf16)
    low = (rest - middle.astype(f32)).astype(bf16)
    return high.astype(f32), middle.astype(f32), low.astype(f32)


def key_bias(length, own, count):
    place = lax.broadcasted_iota(jnp.int32, (count, 128), 0)
    place = (place + own * (count // 2)) & (count - 1)
    return jnp.where(place < length, 0.0, -1000000000.0)


def attend_kernel(info_ref, q_ref, k_ref, v_ref, _c, _l, ctx_ref, lse_ref, *, seq):
    count = q_ref.shape[0]
    lane = lax.broadcasted_iota(jnp.int32, (count, 128), 1)
    bias = key_bias(info_ref[1 + seq], info_ref[0], count)
    query = q_ref[...].astype(f32) * (HEAD_DIM**-0.5)
    keys = k_ref[...].astype(f32)
    values = v_ref[...].astype(f32)
    contexts, sums = [], []
    for head in range(2):
        mine = (lane < 64) if head == 0 else (lane >= 64)
        extra = 64 * (1 - head)
        query_h = jnp.where(mine, query, jnp.where(lane == extra, 1.0, 0.0)).astype(bf16)
        keys_h = jnp.where(mine, keys, jnp.where(lane == extra, bias, 0.0)).astype(bf16)
        values_h = jnp.where(mine, values, 1.0).astype(bf16)
        scores = dot_nt(query_h, keys_h)
        peak = jnp.max(scores, axis=1, keepdims=True)
        exponent = jnp.exp(scores - peak).astype(bf16)
        mixed = dot(exponent, values_h)
        total = pltpu.roll(mixed, 64, 1)
        contexts.append(mixed / total)
        sums.append(peak + jnp.log(mixed))
    low = lane < 64
    ctx_ref[...] = jnp.where(low, contexts[0], contexts[1]).astype(bf16)
    lse_ref[...] = jnp.where(low, sums[1], sums[0])


def attend(info, qkv, seqs, seq, ctx, lse):
    rows, triple = qkv.shape
    count, pairs = rows // seqs, triple // 3 // 128
    block = lambda at: pl.BlockSpec((count, 128), lambda p, info: (seq, p + at * pairs))
    return pl.pallas_call(
        functools.partial(attend_kernel, seq=seq),
        grid_spec=pltpu.PrefetchScalarGridSpec(
            num_scalar_prefetch=1,
            grid=(pairs,),
            in_specs=[block(0), block(1), block(2)] + [pl.BlockSpec(memory_space=pl.ANY)] * 2,
            out_specs=[block(0), block(0)],
        ),
        out_shape=[
            jax.ShapeDtypeStruct((rows, triple // 3), bf16),
            jax.ShapeDtypeStruct((rows, triple // 3), f32),
        ],
        input_output_aliases={4: 0, 5: 1} if seq else {},
        compiler_params=pltpu.CompilerParams(vmem_limit_bytes=14 << 20),
        cost_estimate=pl.CostEstimate(
            flops=9 * 10**9, transcendentals=count * count * pairs * 2, bytes_accessed=count * triple * 4
        ),
        name="attend",
    )(info, qkv, qkv, qkv, ctx, lse)


def attend_back_kernel(
    info_ref, q_ref, k_ref, v_ref, ctx_ref, lse_ref, dctx_ref, earlier_ref, grad_ref, sum_ref, *, seq
):
    count = q_ref.shape[0]
    lane = lax.broadcasted_iota(jnp.int32, (count, 128), 1)
    bias = key_bias(info_ref[1 + seq], info_ref[0], count)
    scale = HEAD_DIM**-0.5
    query = q_ref[...].astype(f32) * scale
    query_low = query.astype(bf16)
    keys_low = k_ref[...]
    keys = keys_low.astype(f32)
    values = v_ref[...].astype(f32)
    grad_low = dctx_ref[...]
    grad = grad_low.astype(f32)
    product = grad * ctx_ref[...].astype(f32)
    lse_parts = three_parts(-lse_ref[...])
    outs = []
    for head in range(2):
        mine = (lane < 64) if head == 0 else (lane >= 64)
        at = lane - 64 * (1 - head)
        ones = jnp.where((at >= 1) & (at <= 3), 1.0, 0.0)

        def spread(parts, first):
            high, middle, low = parts
            value = jnp.where(at == 2, middle, jnp.where(at == 3, low, 0.0))
            return jnp.where(at == 1, high, jnp.where(at == 0, first, value))

        query_h = jnp.where(mine, query, spread(lse_parts, 1.0)).astype(bf16)
        keys_h = jnp.where(mine, keys, jnp.where(at == 0, bias, ones)).astype(bf16)
        inner = -jnp.sum(jnp.where(mine, product, 0.0), axis=1, keepdims=True)
        inner = jnp.broadcast_to(inner, (count, 128))
        grad_h = jnp.where(mine, grad, spread(three_parts(inner), 0.0)).astype(bf16)
        values_h = jnp.where(mine, values, ones).astype(bf16)
        probs = jnp.exp(dot_nt(keys_h, query_h))
        grad_probs = dot_nt(values_h, grad_h)
        grad_scores = (probs * grad_probs).astype(bf16)
        grad_values = dot(probs.astype(bf16), grad_low)
        grad_keys = dot(grad_scores, query_low)
        grad_query = dot_tn(grad_scores, keys_low) * scale
        outs.append((grad_query, grad_keys, grad_values))
    low = lane < 64
    for c, (first, second) in enumerate(zip(outs[0], outs[1])):
        at = pl.multiple_of((c * pl.num_programs(0) + pl.program_id(0)) * 128, 128)
        both = jnp.where(low, first, second).astype(bf16)
        grad_ref[:, pl.ds(at, 128)] = both
        total = jnp.sum(both.astype(f32), axis=0, keepdims=True)
        sum_ref[:, pl.ds(at, 128)] = jnp.broadcast_to(total, (8, 128))


def attend_back(info, qkv, ctx, lse, grad_ctx, seqs, seq, earlier):
    rows, triple = qkv.shape
    count, pairs = rows // seqs, triple // 3 // 128
    block = lambda at: pl.BlockSpec((count, 128), lambda p, info: (seq, p + at * pairs))
    return pl.pallas_call(
        functools.partial(attend_back_kernel, seq=seq),
        grid_spec=pltpu.PrefetchScalarGridSpec(
            num_scalar_prefetch=1,
            grid=(pairs,),
            in_specs=[block(0), block(1), block(2), block(0), block(0), block(0)]
            + [pl.BlockSpec(memory_space=pl.ANY)],
            out_specs=[
                pl.BlockSpec((count, triple), lambda p, info: (seq, 0)),
                pl.BlockSpec((8, triple), lambda p, info: (0, 0)),
            ],
        ),
        out_shape=[
            jax.ShapeDtypeStruct((rows, triple), bf16),
            jax.ShapeDtypeStruct((8, triple), f32),
        ],
        input_output_aliases={7: 0} if seq else {},
        compiler_params=pltpu.CompilerParams(vmem_limit_bytes=24 << 20),
        cost_estimate=pl.CostEstimate(
            flops=16 * 10**9, transcendentals=count * count * pairs * 2, bytes_accessed=count * triple * 5
        ),
        name="attend_back",
    )(info, qkv, qkv, qkv, ctx, lse, grad_ctx, earlier)


def gelu_and_slope(value):
    size = jnp.abs(value)
    near = 1.0 / (1.0 + (0.3275911 * 0.7071067811865476) * size)
    bell = jnp.exp(-0.5 * (value * value))
    poly = 0.5 * 1.061405429
    poly = poly * near + 0.5 * -1.453152027
    poly = poly * near + 0.5 * 1.421413741
    poly = poly * near + 0.5 * -0.284496736
    poly = poly * near + 0.5 * 0.254829592
    tail = poly * near * bell
    phi = jnp.where(value >= 0, 1.0 - tail, tail)
    return value * phi, phi + value * (bell * 0.3989422804014327)


def up_kernel(h_ref, w_ref, b_ref, _g, _s, g_ref, s_ref):
    rows = h_ref.shape[0]
    step = 256
    for at in range(0, rows, step):
        part = pl.ds(at, step)
        before = dot(h_ref[part, :], w_ref[...]) + b_ref[...]
        hidden, slope = gelu_and_slope(before)
        g_ref[part, :] = hidden.astype(bf16)
        s_ref[part, :] = slope.astype(bf16)


def up(first_low, w_in, b_in, part, hidden, slope):
    rows, width = first_low.shape
    units = w_in.shape[1]
    step = 512
    steps = units // step // 2
    column = lambda size: pl.BlockSpec((size, step), lambda i: (0, i + part * steps))
    return pl.pallas_call(
        up_kernel,
        grid=(steps,),
        in_specs=[pl.BlockSpec((rows, width), lambda i: (0, 0)), column(width), column(1)]
        + [pl.BlockSpec(memory_space=pl.ANY)] * 2,
        out_specs=[column(rows)] * 2,
        out_shape=[jax.ShapeDtypeStruct((rows, units), bf16)] * 2,
        input_output_aliases={3: 0, 4: 1} if part else {},
        compiler_params=pltpu.CompilerParams(vmem_limit_bytes=18 << 20),
        cost_estimate=pl.CostEstimate(
            flops=9 * 10**9, transcendentals=rows * units // 2, bytes_accessed=rows * units * 2
        ),
        name="up",
    )(first_low, w_in, b_in, hidden, slope)


def swap(value, even, odd):
    pairs = [(i, i ^ (odd if i & BIT_CORE else even)) for i in range(PLACES)]
    return lax.ppermute(value, BOTH, pairs)


def slots(me):
    core = (me >> 1) & 1
    for other in (0, 1):
        along = jnp.where((core ^ other) == 0, BIT_X, BIT_Y)
        across = (BIT_X + BIT_Y) - along
        for part, bits in enumerate((0, along, across, BIT_X + BIT_Y)):
            for k in range(4):
                yield other, part, k, me ^ (other * BIT_CORE) ^ bits ^ (k * BIT_Z)


def window(ref, move, place):
    _, rows, _, columns, _, step, start, wide = move
    row = pl.multiple_of((place >> 1 if wide else place) * step, 16)
    if not wide:
        return ref.at[pl.ds(row, rows), :]
    column = pl.multiple_of(start + (place & 1) * columns, 128)
    return ref.at[pl.ds(row, rows), pl.ds(column, columns)]


def place_kernel(me_ref, *refs, moves, outs):
    ins, wholes, sems = refs[:8], refs[8 : 8 + outs], refs[8 + outs]
    for other, part, k, place in slots(me_ref[0]):
        for move in moves:
            row, rows, column, columns, to = move[:5]
            pltpu.make_async_copy(
                ins[4 * other + part].at[k, pl.ds(row, rows), pl.ds(column, columns)],
                window(wholes[to], move, place),
                sems.at[to],
            ).start()
    for to in range(outs):
        pltpu.make_async_copy(wholes[to], wholes[to], sems.at[to]).wait()


def spread_kernel(me_ref, *refs, moves, ins):
    wholes, halves, sems = refs[:ins], refs[ins : ins + 2], refs[ins + 2]
    for other, part, k, place in slots(me_ref[0]):
        for move in moves:
            row, rows, column, columns, to = move[:5]
            pltpu.make_async_copy(
                window(wholes[to], move, place),
                halves[other].at[part, k, pl.ds(row, rows), pl.ds(column, columns)],
                sems.at[other],
            ).start()
    for other in (0, 1):
        pltpu.make_async_copy(halves[other], halves[other], sems.at[other]).wait()


anywhere = pl.BlockSpec(memory_space=pltpu.HBM)
on_core = pl.BlockSpec(memory_space=pltpu.VMEM)


def place(me, parts, moves, shapes):
    return pl.pallas_call(
        functools.partial(place_kernel, moves=moves, outs=len(shapes)),
        in_specs=[pl.BlockSpec(memory_space=pltpu.SMEM)] + [anywhere] * 8,
        out_specs=[on_core] * len(shapes),
        out_shape=[jax.ShapeDtypeStruct(shape, bf16) for shape in shapes],
        compiler_params=pltpu.CompilerParams(vmem_limit_bytes=8 << 20),
        cost_estimate=pl.CostEstimate(
            flops=0, transcendentals=0, bytes_accessed=4 * sum(a * b for a, b in shapes)
        ),
        scratch_shapes=[pltpu.SemaphoreType.DMA((len(shapes),))],
        name="place",
    )(me, *parts)


def spread(me, wholes, moves, rows, columns):
    return pl.pallas_call(
        functools.partial(spread_kernel, moves=moves, ins=len(wholes)),
        in_specs=[pl.BlockSpec(memory_space=pltpu.SMEM)] + [anywhere] * len(wholes),
        out_specs=[on_core] * 2,
        out_shape=[jax.ShapeDtypeStruct((4, 4, rows, columns), bf16)] * 2,
        compiler_params=pltpu.CompilerParams(vmem_limit_bytes=8 << 20),
        cost_estimate=pl.CostEstimate(
            flops=0, transcendentals=0, bytes_accessed=128 * rows * columns
        ),
        scratch_shapes=[pltpu.SemaphoreType.DMA((2,))],
        name="spread",
    )(me, *wholes)


def lines_kernel(v_ref, lines_ref, b_ref, *, count, wide):
    places = v_ref.shape[0] // 16
    for place in range(places):
        line = v_ref[pl.ds(place * 16, 16), :].astype(f32)[0:1]
        to = (place % 2) * (places // 2) + place // 2
        starts = [0, count] + [2 * count + wide + i * count for i in range(6)]
        for i, start in enumerate(starts):
            lines_ref[i : i + 1, to * count : (to + 1) * count] = line[:, start : start + count]
        b_ref[:, to * wide : (to + 1) * wide] = line[:, 2 * count : 2 * count + wide]


def unpack_lines(vector_rows, count, wide):
    places = vector_rows.shape[0] // 16
    return pl.pallas_call(
        functools.partial(lines_kernel, count=count, wide=wide),
        out_shape=[
            jax.ShapeDtypeStruct((8, places * count), f32),
            jax.ShapeDtypeStruct((1, places * wide), f32),
        ],
        name="lines",
    )(vector_rows)


def shares_kernel(sums_ref, b_ref, lines_ref, out_ref, held_ref, *, count, wide, width):
    held_ref[...] = jnp.zeros(held_ref.shape, f32)
    places = held_ref.shape[0] // 16
    for place in range(places):
        at = slice(place * 16, place * 16 + 1)
        to = (place % 2) * (places // 2) + place // 2
        own = slice(to * count, (to + 1) * count)
        last = slice(2 * width + to * count, 2 * width + (to + 1) * count)
        held_ref[at, :count] = sums_ref[0:1, own]
        held_ref[at, count : 2 * count] = sums_ref[0:1, last]
        held_ref[at, 2 * count : 2 * count + wide] = b_ref[:, to * wide : (to + 1) * wide]
        for i in range(6):
            start = 2 * count + wide + i * count
            held_ref[at, start : start + count] = lines_ref[i : i + 1, own]
    out_ref[...] = held_ref[...].astype(bf16)


def pack_shares(sums, b_sum, lines, places, columns, count, wide):
    width = lines.shape[1]
    return pl.pallas_call(
        functools.partial(shares_kernel, count=count, wide=wide, width=width),
        out_shape=jax.ShapeDtypeStruct((places * 16, columns), bf16),
        scratch_shapes=[pltpu.VMEM((places * 16, columns), f32)],
        name="shares",
    )(sums, b_sum, lines)


def move_list(row, blocks, vectors=None):
    moves, at = [], -row
    for to, column, columns, start in blocks:
        at = at if column else at + row
        moves.append((at, row, column, columns, to, row, start, True))
    if vectors:
        moves.append((at + row, 16, 0, blocks[0][2], vectors, 16, 0, False))
    return tuple(moves)


def sync(*values):
    return lax.optimization_barrier(values)


def along_z(shard, direct):
    return [shard] + [swap(shard, BIT_Z * k, BIT_Z * k) for k in (1, 2, 3) if direct]


def far_z(shard, direct):
    return [shard] + [swap(shard, 2 * BIT_Z, 2 * BIT_Z) for _ in (0,) if direct]


def near_z(held, direct):
    if not direct:
        return held
    pair = jnp.stack(held)
    got = swap(pair, BIT_Z, BIT_Z)
    return [pair[0], got[0], pair[1], got[1]]


class Gather:
    def __init__(self, me, group, moves, shapes, direct, early=False):
        self.me, self.moves, self.shapes, self.direct = me, moves, shapes, direct
        self.early = early
        self.held, self.stage = group, 0

    def step(self):
        self.stage += 1
        held = self.held
        if not self.direct:
            return
        if self.stage == 1:
            group = jnp.stack(held)
            self.held = [group, swap(group, BIT_X, BIT_Y), swap(group, BIT_Y, BIT_X)]
            if self.early:
                self.held.append(swap(group, BIT_CORE, BIT_CORE))
        elif self.stage == 2:
            corner = swap(held[1], BIT_Y, BIT_X)
            got = held[3:] + [swap(part, BIT_CORE, BIT_CORE) for part in held[len(held) - 3 : 3]]
            self.held = held[:3] + [corner] + got
        else:
            self.held = held + [swap(held[3], BIT_CORE, BIT_CORE)]

    def whole(self):
        if self.direct:
            return place(self.me, self.held, self.moves, self.shapes)
        everything = lax.all_gather(self.held[0], BOTH, axis=0)
        places = everything.shape[0]
        wholes = []
        for to, shape in enumerate(self.shapes):
            pieces = []
            for row, rows, column, columns, at, _, _, wide in self.moves:
                if at != to:
                    continue
                piece = everything[:, row : row + rows, column : column + columns]
                if wide:
                    piece = piece.reshape(places // 2, 2, rows, columns).transpose(0, 2, 1, 3)
                    pieces.append(piece.reshape(places // 2 * rows, 2 * columns))
                else:
                    pieces.append(piece.reshape(shape))
            wholes.append(jnp.concatenate(pieces, axis=1))
        return wholes


def add_low(*parts):
    return sum(part.astype(f32) for part in parts).astype(bf16)


class Reduce:
    def __init__(self, me, wholes, moves, rows, columns, direct, folded=False):
        self.direct, self.stage, self.folded = direct, 0, folded
        if direct:
            self.held = spread(me, wholes, moves, rows, columns)
            return
        pieces = []
        for _, count, _, wide_columns, to, step, start, wide in moves:
            whole = wholes[to]
            if wide:
                whole = whole[:, start : start + 2 * wide_columns]
                whole = whole.reshape(-1, count, 2, wide_columns).transpose(0, 2, 1, 3)
            pieces.append(whole.reshape(-1, count, wide_columns))
        self.held = [jnp.concatenate(pieces, axis=1)]

    def step(self):
        self.stage += 1
        held = self.held
        if not self.direct:
            return
        if self.stage == 1:
            self.held = [held[0], swap(held[1], BIT_CORE, BIT_CORE)]
        elif self.stage == 2:
            total = [add_low(held[0][at], held[1][at]) for at in range(4)]
            self.held = total[:2] + [swap(total[at], BIT_Y, BIT_X) for at in (2, 3)]
        elif self.stage == 3:
            group, near, far, corner = held
            self.held = [group, far, swap(add_low(near, corner), BIT_X, BIT_Y)]
        elif self.folded and self.stage == 4:
            group = add_low(*held)
            self.held = [group[:2], swap(group[2:], 2 * BIT_Z, 2 * BIT_Z)]
        elif self.folded:
            group = add_low(*held)
            self.held = [group[0], swap(group[1], BIT_Z, BIT_Z)]
        else:
            group = add_low(*held)
            self.held = [group[0]] + [swap(group[k], BIT_Z * k, BIT_Z * k) for k in (1, 2, 3)]

    def shard(self):
        if not self.direct:
            return lax.psum_scatter(self.held[0], BOTH, scatter_dimension=0, tiled=True)[
                0
            ].astype(f32)
        return sum(part.astype(f32) for part in self.held)


def shards(
    tokens, lengths, w_qkv, qkv_bias, w_out, w_in, b_in, w_down, norm_gains, row_biases, cotangent, direct
):
    half_len, seq_count, width = tokens.shape
    own = lax.axis_index("tensor")
    me = (lax.axis_index("dp") * 2 + own).astype(jnp.int32).reshape(1)
    seqs = seq_count // 2
    row = w_qkv.shape[1]
    local_width, local_units = w_qkv.shape[2], w_in.shape[1]
    count = qkv_bias.shape[1]
    units = 2 * local_units
    places = width // row * 2
    total_rows = seqs * 2 * half_len

    def trade(value):
        return lax.ppermute(value, "tensor", [(0, 1), (1, 0)])

    def split_rows(value):
        by_seq = jnp.swapaxes(value, 0, 1)
        kept = lax.dynamic_slice_in_dim(by_seq, own * seqs, seqs, 0)
        return kept, lax.dynamic_slice_in_dim(by_seq, (1 - own) * seqs, seqs, 0)

    def to_rows(value):
        kept, sent = split_rows(value)
        return [kept, trade(sent)]

    def as_rows(halves):
        return jnp.stack(halves, axis=1).reshape(total_rows, width)

    def from_rows(kept, got, kind):
        first = jnp.where(own == 0, kept, got)
        second = jnp.where(own == 0, got, kept)
        return jnp.swapaxes(jnp.concatenate([first, second], axis=0), 0, 1).astype(kind)

    def pack(pieces, kind):
        flat = jnp.concatenate([piece.reshape(piece.shape[0], -1) for piece in pieces], axis=1)
        flat = jnp.pad(flat, ((0, 0), (0, local_width - flat.shape[1])))
        return jnp.pad(flat[:, None, :], ((0, 0), (0, 15), (0, 0))).astype(kind)

    vectors = pack(
        [qkv_bias[None], b_in[None], norm_gains[None], row_biases[None]], bf16
    ).reshape(16, local_width)
    attn_shard = jnp.concatenate([w_qkv.reshape(3 * row, local_width), vectors], axis=0)
    qkv_blocks = [(0, 0, local_width, c * width) for c in range(3)]
    qkv_moves = move_list(row, qkv_blocks, 1)
    upper_moves = move_list(row, [(0, 0, local_units, 0), (1, local_units, local_width, 0)])
    mlp_moves = move_list(row, [(0, 0, local_units, 0)])
    out_moves = move_list(row, [(0, 0, local_width, 0)])
    attn_shapes = [(width, 3 * width), (places * 16, local_width)]

    attn_shard, tokens = sync(attn_shard, tokens)
    attn = Gather(me, along_z(attn_shard, direct), qkv_moves, attn_shapes, direct, early=True)
    kept, sent = split_rows(tokens)
    got = [trade(sent[:1])]
    over, under = jnp.concatenate([w_in, w_out.T], axis=1), w_down.T
    attn.held, over, under, kept, got, sent = sync(attn.held, over, under, kept, got, sent)
    attn.step()
    got.append(trade(sent[1:]))
    over = far_z(over, direct)
    attn.held, over, under, kept, got = sync(attn.held, over, under, kept, got)
    attn.step()
    over = near_z(over, direct)
    under = far_z(under, direct)
    rows = as_rows([kept, jnp.concatenate(got, axis=0)])
    attn.held, over, under, rows = sync(attn.held, over, under, rows)
    upper_shapes = [(width, units), (width, width)]
    upper = Gather(me, over, upper_moves, upper_shapes, direct, early=True)
    attn.step()
    under = near_z(under, direct)
    upper.step()
    lower = Gather(me, under, mlp_moves, [(width, units)], direct)
    wq, vector_rows = attn.whole()
    wide = b_in.shape[0]
    if direct:
        lines, b_in_all = unpack_lines(vector_rows, count, wide)
        bias_pair, gains, shifts = lines[:2], lines[2:4], lines[4:]
    else:
        flat = vector_rows.reshape(places // 2, 2, 16, local_width)[:, :, 0]
        flat = jnp.swapaxes(flat, 0, 1).reshape(places, local_width).astype(f32)

        def vector(at, lines, size):
            piece = flat[:, at : at + lines * size].reshape(places, lines, size)
            return jnp.swapaxes(piece, 0, 1).reshape(lines, places * size)

        bias_pair, b_in_all = vector(0, 2, count), vector(2 * count, 1, wide)
        gains, shifts = vector(2 * count + wide, 2, count), vector(4 * count + wide, 4, count)

    mine_lengths = lax.dynamic_slice_in_dim(lengths, own * seqs, seqs, 0)
    info = jnp.concatenate([own.reshape(1).astype(jnp.int32), mine_lengths])

    qkv_shift = jnp.concatenate([bias_pair[0], jnp.zeros((width,), f32), bias_pair[1]])
    qkv = (dot(rows, wq) + qkv_shift).astype(bf16)
    upper.held, lower.held, qkv = sync(upper.held, lower.held, qkv)
    upper.step()
    lower.step()
    ctx, lse = attend(info, qkv, seqs, 0, qkv, qkv)
    for seq in range(1, seqs):
        upper.held, ctx, lse = sync(upper.held, ctx, lse)
        if seq == 1:
            upper.step()
        ctx, lse = attend(info, qkv, seqs, seq, ctx, lse)
    upper.held, lower.held, ctx, cotangent = sync(upper.held, lower.held, ctx, cotangent)
    lower.step()
    grad_halves = to_rows(cotangent)
    wi, wo = upper.whole()
    attended = dot_nt(ctx, wo)
    first, normed_one, inverse_one = norm_forward(
        rows.astype(f32) + attended + shifts[0], gains[0], shifts[1]
    )
    first_low = first.astype(bf16)
    hidden, slope = up(first_low, wi, b_in_all, 0, first_low, first_low)
    lower.held, hidden, slope = sync(lower.held, hidden, slope)
    lower.step()
    hidden, slope = up(first_low, wi, b_in_all, 1, hidden, slope)
    lower.held, hidden, grad_halves = sync(lower.held, hidden, grad_halves)
    (wd,) = lower.whole()
    mixed = dot_nt(hidden, wd)
    output, normed_two, inverse_two = norm_forward(first + mixed + shifts[2], gains[1], shifts[3])

    grad_output = as_rows(grad_halves).astype(f32)
    grad_gain_two = jnp.sum(grad_output * normed_two, axis=0)
    grad_shift_two = jnp.sum(grad_output, axis=0)
    grad_second = norm_backward(grad_output, normed_two, inverse_two, gains[1])
    grad_down_bias = jnp.sum(grad_second, axis=0)
    mixed_grad = grad_second.astype(bf16)
    grad_wd = dot_tn(mixed_grad, hidden).astype(bf16)
    down = Reduce(me, [grad_wd], mlp_moves, row, local_units, direct)
    down.held, mixed_grad, output = sync(down.held, mixed_grad, output.astype(bf16))
    down.step()
    by_half = output.reshape(seqs, 2, half_len, width)
    out_halves = [by_half[:, 0], trade(by_half[:, 1])]
    grad_before = (dot(mixed_grad, wd) * slope.astype(f32)).astype(bf16)
    down.held, grad_before = sync(down.held, grad_before)
    down.step()
    grad_in_bias = jnp.sum(grad_before, axis=0, dtype=f32)
    grad_wi = dot_tn(first_low, grad_before).astype(bf16)
    into = Reduce(me, [grad_wi], mlp_moves, row, local_units, direct, folded=True)
    down.held, into.held, grad_before, out_halves = sync(
        down.held, into.held, grad_before, out_halves
    )
    down.step()
    into.step()
    grad_first = dot_nt(grad_before, wi) + grad_second
    grad_gain_one = jnp.sum(grad_first * normed_one, axis=0)
    grad_shift_one = jnp.sum(grad_first, axis=0)
    grad_resid = norm_backward(grad_first, normed_one, inverse_one, gains[0])
    grad_out_bias = jnp.sum(grad_resid, axis=0)
    attn_grad = grad_resid.astype(bf16)
    down.held, into.held, attn_grad = sync(down.held, into.held, attn_grad)
    down.step()
    into.step()
    grad_wo = dot_tn(attn_grad, ctx).astype(bf16)
    outer = Reduce(me, [grad_wo], out_moves, row, local_width, direct)
    grad_ctx = dot(attn_grad, wo).astype(bf16)
    count_rows = total_rows // seqs
    grad_triple, sums = attend_back(info, qkv, ctx, lse, grad_ctx, seqs, 0, qkv)
    token_halves = []

    def token_grads(seq):
        mine = slice(seq * count_rows, (seq + 1) * count_rows)
        value = dot_nt(grad_triple[mine], wq) + grad_resid[mine]
        return value[:half_len], value[half_len:].astype(bf16)

    for seq in range(1, seqs):
        down.held, into.held, outer.held, token_halves, grad_triple = sync(
            down.held, into.held, outer.held, token_halves, grad_triple
        )
        if seq == 1:
            into.step()
            outer.step()
        kept, sent = token_grads(seq - 1)
        grad_triple, kept, sent = sync(grad_triple, kept, sent)
        token_halves.append([kept, trade(sent)])
        grad_triple, more = attend_back(info, qkv, ctx, lse, grad_ctx, seqs, seq, grad_triple)
        sums = sums + more
    into.held, outer.held, token_halves, grad_triple = sync(
        into.held, outer.held, token_halves, grad_triple
    )
    into.step()
    outer.step()
    kept, sent = token_grads(seqs - 1)
    grad_triple, kept, sent = sync(grad_triple, kept, sent)
    token_halves.append([kept, trade(sent)])
    grad_wq = dot_tn(rows, grad_triple).astype(bf16)

    grad_lines = [
        grad_gain_one, grad_gain_two, grad_out_bias, grad_shift_one, grad_down_bias, grad_shift_two
    ]
    if direct:
        grad_vectors = pack_shares(
            sums, grad_in_bias[None], jnp.stack(grad_lines), places, local_width, count, wide
        )
    else:

        def shares(value, lines):
            size = value.size // lines // places
            piece = value.reshape(lines, 2, places // 2, size)
            return piece.transpose(2, 1, 0, 3).reshape(places, lines * size)

        grad_pair = jnp.stack([sums[0, :width], sums[0, 2 * width :]])
        grad_vectors = pack(
            [shares(grad_pair, 2), shares(grad_in_bias, 1), shares(jnp.stack(grad_lines), 6)], bf16
        ).reshape(places * 16, local_width)
    triple = Reduce(
        me, [grad_wq, grad_vectors], qkv_moves, 3 * row + 16, local_width, direct
    )
    triple.held, into.held, outer.held = sync(triple.held, into.held, outer.held)
    triple.step()
    into.step()
    outer.step()
    triple.held, into.held, outer.held, token_halves = sync(
        triple.held, into.held, outer.held, token_halves
    )
    triple.step()
    outer.step()
    triple.held, out_halves, down.held, into.held, outer.held = sync(
        triple.held, out_halves, down.held, into.held, outer.held
    )
    triple.step()
    out = from_rows(*out_halves, bf16)
    triple.held, token_halves, out = sync(triple.held, token_halves, out)
    triple.step()
    d_tokens = from_rows(
        jnp.stack([kept for kept, _ in token_halves]),
        jnp.stack([got for _, got in token_halves]).astype(f32),
        f32,
    )
    grad_down = down.shard().T
    grad_in = into.shard()
    grad_out = outer.shard().T
    attn_piece = triple.shard()
    grad_qkv = attn_piece[: 3 * row].reshape(3, row, local_width)
    line = attn_piece[3 * row]

    def cut(at, lines, size):
        return line[at : at + lines * size].reshape(lines, size)

    return (
        out,
        d_tokens,
        grad_qkv,
        cut(0, 2, count),
        grad_out,
        grad_in,
        cut(2 * count, 1, wide)[0],
        grad_down,
        cut(2 * count + wide, 2, count),
        cut(4 * count + wide, 4, count),
    )


def solution(mesh):
    placed = (
        P("tensor", "dp", None),
        P("dp"),
        P(None, "dp", "tensor"),
        P(None, ("tensor", "dp")),
        P("tensor", "dp"),
        P("dp", "tensor"),
        P(("tensor", "dp")),
        P("tensor", "dp"),
        P(None, ("tensor", "dp")),
        P(None, ("tensor", "dp")),
        P("tensor", "dp", None),
    )
    direct = mesh.shape["tensor"] == 2 and mesh.shape["dp"] * 2 == PLACES
    return jax.shard_map(
        functools.partial(shards, direct=direct),
        mesh=mesh,
        in_specs=placed,
        out_specs=(
            P("tensor", "dp", None),
            P("tensor", "dp", None),
            P(None, "dp", "tensor"),
            P(None, ("tensor", "dp")),
            P("tensor", "dp"),
            P("dp", "tensor"),
            P(("tensor", "dp")),
            P("tensor", "dp"),
            P(None, ("tensor", "dp")),
            P(None, ("tensor", "dp")),
        ),
        check_vma=False,
    )
```

```python
import functools

import jax
import jax.numpy as jnp
from jax import lax
from jax.experimental import pallas as pl
from jax.experimental.pallas import tpu as pltpu
from jax.sharding import PartitionSpec as P

HEAD_DIM = 64
BOTH = ("dp", "tensor")
BIT_Y, BIT_CORE, BIT_X, BIT_Z = 1, 2, 4, 8
PLACES = 32

norm_eps = 1e-12
bf16 = jnp.bfloat16
f32 = jnp.float32


def norm_backward(grad, normed, inverse, gain):
    scaled = grad * gain
    inner = (
        scaled
        - jnp.mean(scaled, axis=-1, keepdims=True)
        - normed * jnp.mean(scaled * normed, axis=-1, keepdims=True)
    )
    return inner * inverse


def dot(left, right):
    return jnp.dot(left, right, preferred_element_type=f32)


def dot_nt(left, right):
    return lax.dot_general(left, right, (((1,), (1,)), ((), ())), preferred_element_type=f32)


def dot_tn(left, right):
    return lax.dot_general(left, right, (((0,), (0,)), ((), ())), preferred_element_type=f32)


def three_parts(value):
    high = value.astype(bf16)
    rest = value - high.astype(f32)
    middle = rest.astype(bf16)
    low = (rest - middle.astype(f32)).astype(bf16)
    return high.astype(f32), middle.astype(f32), low.astype(f32)


def key_bias(length, own, count):
    place = lax.broadcasted_iota(jnp.int32, (count, 128), 0)
    place = (place + own * (count // 2)) & (count - 1)
    return jnp.where(place < length, 0.0, -1000000000.0)


def attend_kernel(info_ref, q_ref, k_ref, v_ref, _c, _l, ctx_ref, lse_ref, *, seq):
    count = q_ref.shape[0]
    lane = lax.broadcasted_iota(jnp.int32, (count, 128), 1)
    bias = key_bias(info_ref[1 + seq], info_ref[0], count)
    query = q_ref[...].astype(f32) * (HEAD_DIM**-0.5)
    keys = k_ref[...].astype(f32)
    values = v_ref[...].astype(f32)
    contexts, sums = [], []
    for head in range(2):
        mine = (lane < 64) if head == 0 else (lane >= 64)
        extra = 64 * (1 - head)
        query_h = jnp.where(mine, query, jnp.where(lane == extra, 1.0, 0.0)).astype(bf16)
        keys_h = jnp.where(mine, keys, jnp.where(lane == extra, bias, 0.0)).astype(bf16)
        values_h = jnp.where(mine, values, 1.0).astype(bf16)
        scores = dot_nt(query_h, keys_h)
        peak = jnp.max(scores, axis=1, keepdims=True)
        exponent = jnp.exp(scores - peak).astype(bf16)
        mixed = dot(exponent, values_h)
        total = pltpu.roll(mixed, 64, 1)
        contexts.append(mixed / total)
        sums.append(peak + jnp.log(mixed))
    low = lane < 64
    ctx_ref[...] = jnp.where(low, contexts[0], contexts[1]).astype(bf16)
    lse_ref[...] = jnp.where(low, sums[1], sums[0])


def attend(info, qkv, seqs, seq, ctx, lse):
    rows, triple = qkv.shape
    count, pairs = rows // seqs, triple // 3 // 128
    block = lambda at: pl.BlockSpec((count, 128), lambda p, info: (seq, p + at * pairs))
    return pl.pallas_call(
        functools.partial(attend_kernel, seq=seq),
        grid_spec=pltpu.PrefetchScalarGridSpec(
            num_scalar_prefetch=1,
            grid=(pairs,),
            in_specs=[block(0), block(1), block(2)] + [pl.BlockSpec(memory_space=pl.ANY)] * 2,
            out_specs=[block(0), block(0)],
        ),
        out_shape=[
            jax.ShapeDtypeStruct((rows, triple // 3), bf16),
            jax.ShapeDtypeStruct((rows, triple // 3), f32),
        ],
        input_output_aliases={4: 0, 5: 1} if seq else {},
        compiler_params=pltpu.CompilerParams(vmem_limit_bytes=14 << 20),
        cost_estimate=pl.CostEstimate(
            flops=9 * 10**9, transcendentals=count * count * pairs * 2, bytes_accessed=count * triple * 4
        ),
        name="attend",
    )(info, qkv, qkv, qkv, ctx, lse)


def attend_back_kernel(
    info_ref, q_ref, k_ref, v_ref, ctx_ref, lse_ref, dctx_ref, earlier_ref, grad_ref, sum_ref, *, seq
):
    count = q_ref.shape[0]
    lane = lax.broadcasted_iota(jnp.int32, (count, 128), 1)
    bias = key_bias(info_ref[1 + seq], info_ref[0], count)
    scale = HEAD_DIM**-0.5
    query = q_ref[...].astype(f32) * scale
    query_low = query.astype(bf16)
    keys_low = k_ref[...]
    keys = keys_low.astype(f32)
    values = v_ref[...].astype(f32)
    grad_low = dctx_ref[...]
    grad = grad_low.astype(f32)
    product = grad * ctx_ref[...].astype(f32)
    lse_parts = three_parts(-lse_ref[...])
    outs = []
    for head in range(2):
        mine = (lane < 64) if head == 0 else (lane >= 64)
        at = lane - 64 * (1 - head)
        ones = jnp.where((at >= 1) & (at <= 3), 1.0, 0.0)

        def spread(parts, first):
            high, middle, low = parts
            value = jnp.where(at == 2, middle, jnp.where(at == 3, low, 0.0))
            return jnp.where(at == 1, high, jnp.where(at == 0, first, value))

        query_h = jnp.where(mine, query, spread(lse_parts, 1.0)).astype(bf16)
        keys_h = jnp.where(mine, keys, jnp.where(at == 0, bias, ones)).astype(bf16)
        inner = -jnp.sum(jnp.where(mine, product, 0.0), axis=1, keepdims=True)
        inner = jnp.broadcast_to(inner, (count, 128))
        grad_h = jnp.where(mine, grad, spread(three_parts(inner), 0.0)).astype(bf16)
        values_h = jnp.where(mine, values, ones).astype(bf16)
        probs = jnp.exp(dot_nt(keys_h, query_h))
        grad_probs = dot_nt(values_h, grad_h)
        grad_scores = (probs * grad_probs).astype(bf16)
        grad_values = dot(probs.astype(bf16), grad_low)
        grad_keys = dot(grad_scores, query_low)
        grad_query = dot_tn(grad_scores, keys_low) * scale
        outs.append((grad_query, grad_keys, grad_values))
    low = lane < 64
    for c, (first, second) in enumerate(zip(outs[0], outs[1])):
        at = pl.multiple_of((c * pl.num_programs(0) + pl.program_id(0)) * 128, 128)
        both = jnp.where(low, first, second).astype(bf16)
        grad_ref[:, pl.ds(at, 128)] = both
        total = jnp.sum(both.astype(f32), axis=0, keepdims=True)
        sum_ref[:, pl.ds(at, 128)] = jnp.broadcast_to(total, (8, 128))


def attend_back(info, qkv, ctx, lse, grad_ctx, seqs, seq, earlier):
    rows, triple = qkv.shape
    count, pairs = rows // seqs, triple // 3 // 128
    block = lambda at: pl.BlockSpec((count, 128), lambda p, info: (seq, p + at * pairs))
    return pl.pallas_call(
        functools.partial(attend_back_kernel, seq=seq),
        grid_spec=pltpu.PrefetchScalarGridSpec(
            num_scalar_prefetch=1,
            grid=(pairs,),
            in_specs=[block(0), block(1), block(2), block(0), block(0), block(0)]
            + [pl.BlockSpec(memory_space=pl.ANY)],
            out_specs=[
                pl.BlockSpec((count, triple), lambda p, info: (seq, 0)),
                pl.BlockSpec((8, triple), lambda p, info: (0, 0)),
            ],
        ),
        out_shape=[
            jax.ShapeDtypeStruct((rows, triple), bf16),
            jax.ShapeDtypeStruct((8, triple), f32),
        ],
        input_output_aliases={7: 0} if seq else {},
        compiler_params=pltpu.CompilerParams(vmem_limit_bytes=24 << 20),
        cost_estimate=pl.CostEstimate(
            flops=16 * 10**9, transcendentals=count * count * pairs * 2, bytes_accessed=count * triple * 5
        ),
        name="attend_back",
    )(info, qkv, qkv, qkv, ctx, lse, grad_ctx, earlier)


def gelu_and_slope(value):
    size = jnp.abs(value)
    near = 1.0 / (1.0 + (0.3275911 * 0.7071067811865476) * size)
    bell = jnp.exp(-0.5 * (value * value))
    poly = 0.5 * 1.061405429
    poly = poly * near + 0.5 * -1.453152027
    poly = poly * near + 0.5 * 1.421413741
    poly = poly * near + 0.5 * -0.284496736
    poly = poly * near + 0.5 * 0.254829592
    tail = poly * near * bell
    phi = jnp.where(value >= 0, 1.0 - tail, tail)
    return value * phi, phi + value * (bell * 0.3989422804014327)


def up_kernel(h_ref, w_ref, b_ref, _g, _s, g_ref, s_ref):
    rows = h_ref.shape[0]
    step = 256
    for at in range(0, rows, step):
        part = pl.ds(at, step)
        before = dot(h_ref[part, :], w_ref[...]) + b_ref[...]
        hidden, slope = gelu_and_slope(before)
        g_ref[part, :] = hidden.astype(bf16)
        s_ref[part, :] = slope.astype(bf16)


def up(first_low, w_in, b_in, part, hidden, slope):
    rows, width = first_low.shape
    units = w_in.shape[1]
    step = 512
    steps = units // step // 2
    column = lambda size: pl.BlockSpec((size, step), lambda i: (0, i + part * steps))
    return pl.pallas_call(
        up_kernel,
        grid=(steps,),
        in_specs=[pl.BlockSpec((rows, width), lambda i: (0, 0)), column(width), column(1)]
        + [pl.BlockSpec(memory_space=pl.ANY)] * 2,
        out_specs=[column(rows)] * 2,
        out_shape=[jax.ShapeDtypeStruct((rows, units), bf16)] * 2,
        input_output_aliases={3: 0, 4: 1} if part else {},
        compiler_params=pltpu.CompilerParams(vmem_limit_bytes=18 << 20),
        cost_estimate=pl.CostEstimate(
            flops=9 * 10**9, transcendentals=rows * units // 2, bytes_accessed=rows * units * 2
        ),
        name="up",
    )(first_low, w_in, b_in, hidden, slope)


def normalize(values):
    centered = values - jnp.mean(values, axis=-1, keepdims=True)
    inverse = lax.rsqrt(jnp.mean(centered * centered, axis=-1, keepdims=True) + norm_eps)
    return centered * inverse, inverse


def add_sums(ref, lines):
    @pl.when(pl.program_id(0) == 0)
    def _():
        ref[...] = jnp.zeros(ref.shape, f32)

    for i, line in enumerate(lines):
        ref[i : i + 1, :] += jnp.sum(line, axis=0, keepdims=True)


def out_kernel(ctx_ref, w_ref, x_ref, v_ref, first_ref, low_ref, normed_ref, inverse_ref):
    values = x_ref[...].astype(f32) + dot_nt(ctx_ref[...], w_ref[...]) + v_ref[1:2, :]
    normed, inverse = normalize(values)
    first = normed * v_ref[0:1, :] + v_ref[2:3, :]
    first_ref[...] = first
    low_ref[...] = first.astype(bf16)
    normed_ref[...] = normed
    inverse_ref[...] = jnp.broadcast_to(inverse, inverse_ref.shape)


def down_kernel(
    g_ref, w_ref, first_ref, kept_ref, got_ref, v_ref, out_ref, grad_ref, low_ref, sum_ref
):
    values = first_ref[...] + dot_nt(g_ref[...], w_ref[...]) + v_ref[1:2, :]
    normed, inverse = normalize(values)
    out_ref[...] = (normed * v_ref[0:1, :] + v_ref[2:3, :]).astype(bf16)
    mine = pl.program_id(0) % 2 == 0
    given = jnp.where(mine, kept_ref[0].astype(f32), got_ref[0].astype(f32))
    grad = norm_backward(given, normed, inverse, v_ref[0:1, :])
    grad_ref[...] = grad
    low_ref[...] = grad.astype(bf16)
    add_sums(sum_ref, (given * normed, given, grad))


def back_kernel(
    u_ref, w_ref, second_ref, normed_ref, inverse_ref, v_ref, grad_ref, low_ref, sum_ref
):
    given = dot_nt(u_ref[...], w_ref[...]) + second_ref[...]
    normed = normed_ref[...]
    grad = norm_backward(given, normed, inverse_ref[:, :1], v_ref[0:1, :])
    grad_ref[...] = grad
    low_ref[...] = grad.astype(bf16)
    add_sums(sum_ref, (given * normed, given, grad))


def by_rows(kernel, name, rows, step, ins, outs):
    def spec(shape, kind):
        if kind == "rows":
            return pl.BlockSpec((step, shape[1]), lambda i: (i, 0))
        if kind == "half":
            return pl.BlockSpec((1, step, shape[2]), lambda i: (i // 2, 0, 0))
        return pl.BlockSpec(shape, lambda i: (0, 0))

    shapes = [jax.ShapeDtypeStruct(shape, kind) for shape, kind, _ in outs]
    return pl.pallas_call(
        kernel,
        grid=(rows // step,),
        in_specs=[spec(value.shape, kind) for value, kind in ins],
        out_specs=[spec(shape, kind) for shape, _, kind in outs],
        out_shape=shapes,
        compiler_params=pltpu.CompilerParams(vmem_limit_bytes=30 << 20),
        cost_estimate=pl.CostEstimate(
            flops=2 * rows * ins[1][0].size,
            transcendentals=0,
            bytes_accessed=0,
        ),
        name=name,
    )(*[value for value, _ in ins])


def swap(value, even, odd):
    pairs = [(i, i ^ (odd if i & BIT_CORE else even)) for i in range(PLACES)]
    return lax.ppermute(value, BOTH, pairs)


def slots(me):
    core = (me >> 1) & 1
    for other in (0, 1):
        along = jnp.where((core ^ other) == 0, BIT_X, BIT_Y)
        across = (BIT_X + BIT_Y) - along
        for part, bits in enumerate((0, along, across, BIT_X + BIT_Y)):
            for k in range(4):
                yield other, part, k, me ^ (other * BIT_CORE) ^ bits ^ (k * BIT_Z)


def window(ref, move, place):
    _, rows, _, columns, _, step, start, wide = move
    row = pl.multiple_of((place >> 1 if wide else place) * step, 16)
    if not wide:
        return ref.at[pl.ds(row, rows), :]
    column = pl.multiple_of(start + (place & 1) * columns, 128)
    return ref.at[pl.ds(row, rows), pl.ds(column, columns)]


def place_kernel(me_ref, *refs, moves, outs):
    ins, wholes, sems = refs[:8], refs[8 : 8 + outs], refs[8 + outs]
    for other, part, k, place in slots(me_ref[0]):
        for move in moves:
            row, rows, column, columns, to = move[:5]
            pltpu.make_async_copy(
                ins[4 * other + part].at[k, pl.ds(row, rows), pl.ds(column, columns)],
                window(wholes[to], move, place),
                sems.at[to],
            ).start()
    for to in range(outs):
        pltpu.make_async_copy(wholes[to], wholes[to], sems.at[to]).wait()


def spread_kernel(me_ref, *refs, moves, ins):
    wholes, halves, sems = refs[:ins], refs[ins : ins + 2], refs[ins + 2]
    for other, part, k, place in slots(me_ref[0]):
        for move in moves:
            row, rows, column, columns, to = move[:5]
            pltpu.make_async_copy(
                window(wholes[to], move, place),
                halves[other].at[part, k, pl.ds(row, rows), pl.ds(column, columns)],
                sems.at[other],
            ).start()
    for other in (0, 1):
        pltpu.make_async_copy(halves[other], halves[other], sems.at[other]).wait()


anywhere = pl.BlockSpec(memory_space=pltpu.HBM)
on_core = pl.BlockSpec(memory_space=pltpu.VMEM)


def place(me, parts, moves, shapes):
    return pl.pallas_call(
        functools.partial(place_kernel, moves=moves, outs=len(shapes)),
        in_specs=[pl.BlockSpec(memory_space=pltpu.SMEM)] + [anywhere] * 8,
        out_specs=[on_core] * len(shapes),
        out_shape=[jax.ShapeDtypeStruct(shape, bf16) for shape in shapes],
        compiler_params=pltpu.CompilerParams(vmem_limit_bytes=8 << 20),
        cost_estimate=pl.CostEstimate(
            flops=4 * 10**9, transcendentals=0, bytes_accessed=0
        ),
        scratch_shapes=[pltpu.SemaphoreType.DMA((len(shapes),))],
        name="place",
    )(me, *parts)


def spread(me, wholes, moves, rows, columns):
    return pl.pallas_call(
        functools.partial(spread_kernel, moves=moves, ins=len(wholes)),
        in_specs=[pl.BlockSpec(memory_space=pltpu.SMEM)] + [anywhere] * len(wholes),
        out_specs=[on_core] * 2,
        out_shape=[jax.ShapeDtypeStruct((4, 4, rows, columns), bf16)] * 2,
        compiler_params=pltpu.CompilerParams(vmem_limit_bytes=8 << 20),
        cost_estimate=pl.CostEstimate(
            flops=2 * 10**9, transcendentals=0, bytes_accessed=0
        ),
        scratch_shapes=[pltpu.SemaphoreType.DMA((2,))],
        name="spread",
    )(me, *wholes)


def lines_kernel(v_ref, lines_ref, b_ref, *, count, wide):
    places = v_ref.shape[0] // 16
    for place in range(places):
        line = v_ref[pl.ds(place * 16, 16), :].astype(f32)[0:1]
        to = (place % 2) * (places // 2) + place // 2
        starts = [0, count] + [2 * count + wide + i * count for i in range(6)]
        for i, start in enumerate(starts):
            lines_ref[i : i + 1, to * count : (to + 1) * count] = line[:, start : start + count]
        b_ref[:, to * wide : (to + 1) * wide] = line[:, 2 * count : 2 * count + wide]


def unpack_lines(vector_rows, count, wide):
    places = vector_rows.shape[0] // 16
    return pl.pallas_call(
        functools.partial(lines_kernel, count=count, wide=wide),
        out_shape=[
            jax.ShapeDtypeStruct((8, places * count), f32),
            jax.ShapeDtypeStruct((1, places * wide), f32),
        ],
        name="lines",
    )(vector_rows)


def shares_kernel(sums_ref, b_ref, one_ref, two_ref, out_ref, held_ref, *, count, wide, width):
    held_ref[...] = jnp.zeros(held_ref.shape, f32)
    places = held_ref.shape[0] // 16
    for place in range(places):
        at = slice(place * 16, place * 16 + 1)
        to = (place % 2) * (places // 2) + place // 2
        own = slice(to * count, (to + 1) * count)
        last = slice(2 * width + to * count, 2 * width + (to + 1) * count)
        held_ref[at, :count] = sums_ref[0:1, own]
        held_ref[at, count : 2 * count] = sums_ref[0:1, last]
        held_ref[at, 2 * count : 2 * count + wide] = b_ref[:, to * wide : (to + 1) * wide]
        lines = ((one_ref, 0), (two_ref, 0), (one_ref, 2), (one_ref, 1), (two_ref, 2), (two_ref, 1))
        for i, (ref, line) in enumerate(lines):
            start = 2 * count + wide + i * count
            held_ref[at, start : start + count] = ref[line : line + 1, own]
    out_ref[...] = held_ref[...].astype(bf16)


def pack_shares(sums, b_sum, one, two, places, columns, count, wide):
    width = one.shape[1]
    return pl.pallas_call(
        functools.partial(shares_kernel, count=count, wide=wide, width=width),
        out_shape=jax.ShapeDtypeStruct((places * 16, columns), bf16),
        scratch_shapes=[pltpu.VMEM((places * 16, columns), f32)],
        name="shares",
    )(sums, b_sum, one, two)


def move_list(row, blocks, vectors=None):
    moves, at = [], -row
    for to, column, columns, start in blocks:
        at = at if column else at + row
        moves.append((at, row, column, columns, to, row, start, True))
    if vectors:
        moves.append((at + row, 16, 0, blocks[0][2], vectors, 16, 0, False))
    return tuple(moves)


def sync(*values):
    return lax.optimization_barrier(values)


def along_z(shard, direct):
    return [shard] + [swap(shard, BIT_Z * k, BIT_Z * k) for k in (1, 2, 3) if direct]


def far_z(shard, direct):
    return [shard] + [swap(shard, 2 * BIT_Z, 2 * BIT_Z) for _ in (0,) if direct]


def near_z(held, direct):
    if not direct:
        return held
    pair = jnp.stack(held)
    got = swap(pair, BIT_Z, BIT_Z)
    return [pair[0], got[0], pair[1], got[1]]


class Gather:
    def __init__(self, me, group, moves, shapes, direct, early=False):
        self.me, self.moves, self.shapes, self.direct = me, moves, shapes, direct
        self.early = early
        self.held, self.stage = group, 0

    def step(self):
        self.stage += 1
        held = self.held
        if not self.direct:
            return
        if self.stage == 1:
            group = jnp.stack(held)
            self.held = [group, swap(group, BIT_X, BIT_Y), swap(group, BIT_Y, BIT_X)]
            if self.early:
                self.held.append(swap(group, BIT_CORE, BIT_CORE))
        elif self.stage == 2:
            corner = swap(held[1], BIT_Y, BIT_X)
            got = held[3:] + [swap(part, BIT_CORE, BIT_CORE) for part in held[len(held) - 3 : 3]]
            self.held = held[:3] + [corner] + got
        else:
            self.held = held + [swap(held[3], BIT_CORE, BIT_CORE)]

    def whole(self):
        if self.direct:
            return place(self.me, self.held, self.moves, self.shapes)
        everything = lax.all_gather(self.held[0], BOTH, axis=0)
        places = everything.shape[0]
        wholes = []
        for to, shape in enumerate(self.shapes):
            pieces = []
            for row, rows, column, columns, at, _, _, wide in self.moves:
                if at != to:
                    continue
                piece = everything[:, row : row + rows, column : column + columns]
                if wide:
                    piece = piece.reshape(places // 2, 2, rows, columns).transpose(0, 2, 1, 3)
                    pieces.append(piece.reshape(places // 2 * rows, 2 * columns))
                else:
                    pieces.append(piece.reshape(shape))
            wholes.append(jnp.concatenate(pieces, axis=1))
        return wholes


def add_low(*parts):
    return sum(part.astype(f32) for part in parts).astype(bf16)


class Reduce:
    def __init__(self, me, wholes, moves, rows, columns, direct, folded=False):
        self.direct, self.stage, self.folded = direct, 0, folded
        if direct:
            self.held = spread(me, wholes, moves, rows, columns)
            return
        pieces = []
        for _, count, _, wide_columns, to, step, start, wide in moves:
            whole = wholes[to]
            if wide:
                whole = whole[:, start : start + 2 * wide_columns]
                whole = whole.reshape(-1, count, 2, wide_columns).transpose(0, 2, 1, 3)
            pieces.append(whole.reshape(-1, count, wide_columns))
        self.held = [jnp.concatenate(pieces, axis=1)]

    def step(self):
        self.stage += 1
        held = self.held
        if not self.direct:
            return
        if self.stage == 1:
            self.held = [held[0], swap(held[1], BIT_CORE, BIT_CORE)]
        elif self.stage == 2:
            total = [add_low(held[0][at], held[1][at]) for at in range(4)]
            self.held = total[:2] + [swap(total[at], BIT_Y, BIT_X) for at in (2, 3)]
        elif self.stage == 3:
            group, near, far, corner = held
            self.held = [group, far, swap(add_low(near, corner), BIT_X, BIT_Y)]
        elif self.folded and self.stage == 4:
            group = add_low(*held)
            self.held = [group[:2], swap(group[2:], 2 * BIT_Z, 2 * BIT_Z)]
        elif self.folded:
            group = add_low(*held)
            self.held = [group[0], swap(group[1], BIT_Z, BIT_Z)]
        else:
            group = add_low(*held)
            self.held = [group[0]] + [swap(group[k], BIT_Z * k, BIT_Z * k) for k in (1, 2, 3)]

    def shard(self):
        if not self.direct:
            return lax.psum_scatter(self.held[0], BOTH, scatter_dimension=0, tiled=True)[
                0
            ].astype(f32)
        return sum(part.astype(f32) for part in self.held)


def shards(
    tokens, lengths, w_qkv, qkv_bias, w_out, w_in, b_in, w_down, norm_gains, row_biases, cotangent, direct
):
    half_len, seq_count, width = tokens.shape
    own = lax.axis_index("tensor")
    me = (lax.axis_index("dp") * 2 + own).astype(jnp.int32).reshape(1)
    seqs = seq_count // 2
    row = w_qkv.shape[1]
    local_width, local_units = w_qkv.shape[2], w_in.shape[1]
    count = qkv_bias.shape[1]
    units = 2 * local_units
    places = width // row * 2
    total_rows = seqs * 2 * half_len

    def trade(value):
        return lax.ppermute(value, "tensor", [(0, 1), (1, 0)])

    def split_rows(value):
        by_seq = jnp.swapaxes(value, 0, 1)
        kept = lax.dynamic_slice_in_dim(by_seq, own * seqs, seqs, 0)
        return kept, lax.dynamic_slice_in_dim(by_seq, (1 - own) * seqs, seqs, 0)

    def to_rows(value):
        kept, sent = split_rows(value)
        return [kept, trade(sent)]

    def as_rows(halves):
        return jnp.stack(halves, axis=1).reshape(total_rows, width)

    def from_rows(kept, got, kind):
        first = jnp.where(own == 0, kept, got)
        second = jnp.where(own == 0, got, kept)
        return jnp.swapaxes(jnp.concatenate([first, second], axis=0), 0, 1).astype(kind)

    def pack(pieces, kind):
        flat = jnp.concatenate([piece.reshape(piece.shape[0], -1) for piece in pieces], axis=1)
        flat = jnp.pad(flat, ((0, 0), (0, local_width - flat.shape[1])))
        return jnp.pad(flat[:, None, :], ((0, 0), (0, 15), (0, 0))).astype(kind)

    vectors = pack(
        [qkv_bias[None], b_in[None], norm_gains[None], row_biases[None]], bf16
    ).reshape(16, local_width)
    attn_shard = jnp.concatenate([w_qkv.reshape(3 * row, local_width), vectors], axis=0)
    qkv_blocks = [(0, 0, local_width, c * width) for c in range(3)]
    qkv_moves = move_list(row, qkv_blocks, 1)
    upper_moves = move_list(row, [(0, 0, local_units, 0), (1, local_units, local_width, 0)])
    mlp_moves = move_list(row, [(0, 0, local_units, 0)])
    out_moves = move_list(row, [(0, 0, local_width, 0)])
    attn_shapes = [(width, 3 * width), (places * 16, local_width)]

    attn_shard, tokens = sync(attn_shard, tokens)
    attn = Gather(me, along_z(attn_shard, direct), qkv_moves, attn_shapes, direct)
    kept, sent = split_rows(tokens)
    got = [trade(sent[:1])]
    over, under = jnp.concatenate([w_in, w_out.T], axis=1), w_down.T
    attn.held, over, under, kept, got, sent = sync(attn.held, over, under, kept, got, sent)
    attn.step()
    got.append(trade(sent[1:]))
    over = far_z(over, direct)
    under = far_z(under, direct)
    attn.held, over, under, kept, got = sync(attn.held, over, under, kept, got)
    attn.step()
    over = near_z(over, direct)
    rows = as_rows([kept, jnp.concatenate(got, axis=0)])
    attn.held, over, under, rows = sync(attn.held, over, under, rows)
    upper_shapes = [(width, units), (width, width)]
    upper = Gather(me, over, upper_moves, upper_shapes, direct, early=True)
    attn.step()
    under = near_z(under, direct)
    upper.step()
    lower = Gather(me, under, mlp_moves, [(width, units)], direct)
    wq, vector_rows = attn.whole()
    wide = b_in.shape[0]
    if direct:
        lines, b_in_all = unpack_lines(vector_rows, count, wide)
        bias_pair, gains, shifts = lines[:2], lines[2:4], lines[4:]
    else:
        flat = vector_rows.reshape(places // 2, 2, 16, local_width)[:, :, 0]
        flat = jnp.swapaxes(flat, 0, 1).reshape(places, local_width).astype(f32)

        def vector(at, lines, size):
            piece = flat[:, at : at + lines * size].reshape(places, lines, size)
            return jnp.swapaxes(piece, 0, 1).reshape(lines, places * size)

        bias_pair, b_in_all = vector(0, 2, count), vector(2 * count, 1, wide)
        gains, shifts = vector(2 * count + wide, 2, count), vector(4 * count + wide, 4, count)

    mine_lengths = lax.dynamic_slice_in_dim(lengths, own * seqs, seqs, 0)
    info = jnp.concatenate([own.reshape(1).astype(jnp.int32), mine_lengths])

    upper.held, wq, bias_pair = sync(upper.held, wq, bias_pair)
    upper.step()
    qkv_shift = jnp.concatenate([bias_pair[0], jnp.zeros((width,), f32), bias_pair[1]])
    qkv = (dot(rows, wq) + qkv_shift).astype(bf16)
    lower.held, qkv = sync(lower.held, qkv)
    lower.step()
    ctx, lse = attend(info, qkv, seqs, 0, qkv, qkv)
    for seq in range(1, seqs):
        upper.held, ctx, lse = sync(upper.held, ctx, lse)
        if seq == 1:
            upper.step()
        ctx, lse = attend(info, qkv, seqs, seq, ctx, lse)
    upper.held, lower.held, ctx, cotangent = sync(upper.held, lower.held, ctx, cotangent)
    lower.step()
    grad_halves = to_rows(cotangent)
    wi, wo = upper.whole()
    one_lines = jnp.stack([gains[0], shifts[0], shifts[1]])
    two_lines = jnp.stack([gains[1], shifts[2], shifts[3]])
    wide_rows = (total_rows, width)
    first, first_low, normed_one, inverse_one = by_rows(
        out_kernel,
        "attention_out",
        total_rows,
        half_len,
        [(ctx, "rows"), (wo, "whole"), (rows, "rows"), (one_lines, "whole")],
        [
            (wide_rows, f32, "rows"),
            (wide_rows, bf16, "rows"),
            (wide_rows, f32, "rows"),
            ((total_rows, 128), f32, "rows"),
        ],
    )
    hidden, slope = up(first_low, wi, b_in_all, 0, first_low, first_low)
    lower.held, hidden, slope = sync(lower.held, hidden, slope)
    lower.step()
    hidden, slope = up(first_low, wi, b_in_all, 1, hidden, slope)
    lower.held, hidden, grad_halves = sync(lower.held, hidden, grad_halves)
    (wd,) = lower.whole()
    output, grad_second, mixed_grad, two_sums = by_rows(
        down_kernel,
        "down",
        total_rows,
        half_len,
        [
            (hidden, "rows"),
            (wd, "whole"),
            (first, "rows"),
            (grad_halves[0], "half"),
            (grad_halves[1], "half"),
            (two_lines, "whole"),
        ],
        [
            (wide_rows, bf16, "rows"),
            (wide_rows, f32, "rows"),
            (wide_rows, bf16, "rows"),
            ((8, width), f32, "whole"),
        ],
    )
    by_half = output.reshape(seqs, 2, half_len, width)
    early, late, mixed_grad, hidden = sync(by_half[:1, 1], by_half[1:, 1], mixed_grad, hidden)
    early = trade(early)
    grad_wd = dot_tn(mixed_grad, hidden).astype(bf16)
    down = Reduce(me, [grad_wd], mlp_moves, row, local_units, direct, folded=True)
    down.held, mixed_grad, early, late = sync(down.held, mixed_grad, early, late)
    late = trade(late)
    down.step()
    grad_before = (dot(mixed_grad, wd) * slope.astype(f32)).astype(bf16)
    down.held, grad_before, late = sync(down.held, grad_before, late)
    down.step()
    grad_in_bias = jnp.sum(grad_before, axis=0, dtype=f32)
    grad_wi = dot_tn(first_low, grad_before).astype(bf16)
    into = Reduce(me, [grad_wi], mlp_moves, row, local_units, direct, folded=True)
    into.held, grad_before = sync(into.held, grad_before)
    into.step()
    grad_resid, attn_grad, one_sums = by_rows(
        back_kernel,
        "up_back",
        total_rows,
        half_len,
        [
            (grad_before, "rows"),
            (wi, "whole"),
            (grad_second, "rows"),
            (normed_one, "rows"),
            (inverse_one, "rows"),
            (one_lines, "whole"),
        ],
        [(wide_rows, f32, "rows"), (wide_rows, bf16, "rows"), ((8, width), f32, "whole")],
    )
    grad_wo = dot_tn(attn_grad, ctx).astype(bf16)
    grad_ctx = dot(attn_grad, wo).astype(bf16)
    down.held, into.held, grad_wo, grad_ctx = sync(down.held, into.held, grad_wo, grad_ctx)
    down.step()
    into.step()
    outer = Reduce(me, [grad_wo], out_moves, row, local_width, direct, folded=True)
    outer.step()
    count_rows = total_rows // seqs
    grad_triple, sums = attend_back(info, qkv, ctx, lse, grad_ctx, seqs, 0, qkv)
    token_halves = []

    def token_grads(seq):
        mine = slice(seq * count_rows, (seq + 1) * count_rows)
        value = dot_nt(grad_triple[mine], wq) + grad_resid[mine]
        return value[:half_len], value[half_len:].astype(bf16)

    for seq in range(1, seqs):
        first_held = into.held[:3]
        down.held, first_held, outer.held, token_halves, grad_triple = sync(
            down.held, first_held, outer.held, token_halves, grad_triple
        )
        into.held = first_held + into.held[3:]
        if seq == 1:
            down.step()
            outer.step()
        kept, sent = token_grads(seq - 1)
        grad_triple, kept, sent = sync(grad_triple, kept, sent)
        token_halves.append([kept, trade(sent)])
        grad_triple, more = attend_back(info, qkv, ctx, lse, grad_ctx, seqs, seq, grad_triple)
        sums = sums + more
    down.held, into.held, outer.held, token_halves, grad_triple = sync(
        down.held, into.held, outer.held, token_halves, grad_triple
    )
    into.step()
    grad_wq = dot_tn(rows, grad_triple).astype(bf16)

    if direct:
        grad_vectors = pack_shares(
            sums, grad_in_bias[None], one_sums, two_sums, places, local_width, count, wide
        )
    else:

        def shares(value, lines):
            size = value.size // lines // places
            piece = value.reshape(lines, 2, places // 2, size)
            return piece.transpose(2, 1, 0, 3).reshape(places, lines * size)

        grad_pair = jnp.stack([sums[0, :width], sums[0, 2 * width :]])
        one, two = one_sums, two_sums
        grad_lines = [one[0], two[0], one[2], one[1], two[2], two[1]]
        grad_vectors = pack(
            [shares(grad_pair, 2), shares(grad_in_bias, 1), shares(jnp.stack(grad_lines), 6)], bf16
        ).reshape(places * 16, local_width)
    triple = Reduce(
        me, [grad_wq, grad_vectors], qkv_moves, 3 * row + 16, local_width, direct
    )
    triple.held, grad_triple = sync(triple.held, grad_triple)
    triple.step()
    kept, sent = token_grads(seqs - 1)
    triple.held, into.held, kept, sent = sync(triple.held, into.held, kept, sent)
    triple.step()
    into.step()
    down.step()
    outer.step()
    triple.held, down.held, into.held, outer.held, early, late, by_half = sync(
        triple.held, down.held, into.held, outer.held, early, late, by_half
    )
    triple.step()
    into.step()
    outer.step()
    out = from_rows(by_half[:, 0], jnp.concatenate([early, late]), bf16)
    triple.held, into.held, outer.held, sent, out = sync(
        triple.held, into.held, outer.held, sent, out
    )
    triple.step()
    outer.step()
    token_halves.append([kept, trade(sent)])
    d_tokens = from_rows(
        jnp.stack([kept for kept, _ in token_halves]),
        jnp.stack([got for _, got in token_halves]).astype(f32),
        f32,
    )
    grad_down = down.shard().T
    grad_in = into.shard()
    grad_out = outer.shard().T
    attn_piece = triple.shard()
    grad_qkv = attn_piece[: 3 * row].reshape(3, row, local_width)
    line = attn_piece[3 * row]

    def cut(at, lines, size):
        return line[at : at + lines * size].reshape(lines, size)

    return (
        out,
        d_tokens,
        grad_qkv,
        cut(0, 2, count),
        grad_out,
        grad_in,
        cut(2 * count, 1, wide)[0],
        grad_down,
        cut(2 * count + wide, 2, count),
        cut(4 * count + wide, 4, count),
    )


def solution(mesh):
    placed = (
        P("tensor", "dp", None),
        P("dp"),
        P(None, "dp", "tensor"),
        P(None, ("tensor", "dp")),
        P("tensor", "dp"),
        P("dp", "tensor"),
        P(("tensor", "dp")),
        P("tensor", "dp"),
        P(None, ("tensor", "dp")),
        P(None, ("tensor", "dp")),
        P("tensor", "dp", None),
    )
    direct = mesh.shape["tensor"] == 2 and mesh.shape["dp"] * 2 == PLACES
    return jax.shard_map(
        functools.partial(shards, direct=direct),
        mesh=mesh,
        in_specs=placed,
        out_specs=(
            P("tensor", "dp", None),
            P("tensor", "dp", None),
            P(None, "dp", "tensor"),
            P(None, ("tensor", "dp")),
            P("tensor", "dp"),
            P("dp", "tensor"),
            P(("tensor", "dp")),
            P("tensor", "dp"),
            P(None, ("tensor", "dp")),
            P(None, ("tensor", "dp")),
        ),
        check_vma=False,
    )
```

```python
import functools

import jax
import jax.numpy as jnp
from jax import lax
from jax.experimental import pallas as pl
from jax.experimental.pallas import tpu as pltpu
from jax.sharding import PartitionSpec as P

HEAD_DIM = 64
BOTH = ("dp", "tensor")
BIT_Y, BIT_CORE, BIT_X, BIT_Z = 1, 2, 4, 8
PLACES = 32

norm_eps = 1e-12
bf16 = jnp.bfloat16
f32 = jnp.float32


def norm_backward(grad, normed, inverse, gain):
    scaled = grad * gain
    inner = (
        scaled
        - jnp.mean(scaled, axis=-1, keepdims=True)
        - normed * jnp.mean(scaled * normed, axis=-1, keepdims=True)
    )
    return inner * inverse


def dot(left, right):
    return jnp.dot(left, right, preferred_element_type=f32)


def dot_nt(left, right):
    return lax.dot_general(left, right, (((1,), (1,)), ((), ())), preferred_element_type=f32)


def dot_tn(left, right):
    return lax.dot_general(left, right, (((0,), (0,)), ((), ())), preferred_element_type=f32)


def three_parts(value):
    high = value.astype(bf16)
    rest = value - high.astype(f32)
    middle = rest.astype(bf16)
    low = (rest - middle.astype(f32)).astype(bf16)
    return high.astype(f32), middle.astype(f32), low.astype(f32)


def key_bias(length, own, count):
    place = lax.broadcasted_iota(jnp.int32, (count, 128), 0)
    place = (place + own * (count // 2)) & (count - 1)
    return jnp.where(place < length, 0.0, -1000000000.0)


def attend_kernel(info_ref, q_ref, k_ref, v_ref, _c, _l, ctx_ref, lse_ref, *, seq):
    count = q_ref.shape[0]
    lane = lax.broadcasted_iota(jnp.int32, (count, 128), 1)
    bias = key_bias(info_ref[1 + seq], info_ref[0], count)
    query = q_ref[...].astype(f32) * (HEAD_DIM**-0.5)
    keys = k_ref[...].astype(f32)
    values = v_ref[...].astype(f32)
    contexts, sums = [], []
    for head in range(2):
        mine = (lane < 64) if head == 0 else (lane >= 64)
        extra = 64 * (1 - head)
        query_h = jnp.where(mine, query, jnp.where(lane == extra, 1.0, 0.0)).astype(bf16)
        keys_h = jnp.where(mine, keys, jnp.where(lane == extra, bias, 0.0)).astype(bf16)
        values_h = jnp.where(mine, values, 1.0).astype(bf16)
        scores = dot_nt(query_h, keys_h)
        peak = jnp.max(scores, axis=1, keepdims=True)
        exponent = jnp.exp(scores - peak).astype(bf16)
        mixed = dot(exponent, values_h)
        total = pltpu.roll(mixed, 64, 1)
        contexts.append(mixed / total)
        sums.append(peak + jnp.log(mixed))
    low = lane < 64
    ctx_ref[...] = jnp.where(low, contexts[0], contexts[1]).astype(bf16)
    lse_ref[...] = jnp.where(low, sums[1], sums[0])


def attend(info, qkv, seqs, seq, ctx, lse):
    rows, triple = qkv.shape
    count, pairs = rows // seqs, triple // 3 // 128
    block = lambda at: pl.BlockSpec((count, 128), lambda p, info: (seq, p + at * pairs))
    return pl.pallas_call(
        functools.partial(attend_kernel, seq=seq),
        grid_spec=pltpu.PrefetchScalarGridSpec(
            num_scalar_prefetch=1,
            grid=(pairs,),
            in_specs=[block(0), block(1), block(2)] + [pl.BlockSpec(memory_space=pl.ANY)] * 2,
            out_specs=[block(0), block(0)],
        ),
        out_shape=[
            jax.ShapeDtypeStruct((rows, triple // 3), bf16),
            jax.ShapeDtypeStruct((rows, triple // 3), f32),
        ],
        input_output_aliases={4: 0, 5: 1} if seq else {},
        compiler_params=pltpu.CompilerParams(vmem_limit_bytes=14 << 20),
        cost_estimate=pl.CostEstimate(
            flops=9 * 10**9, transcendentals=count * count * pairs * 2, bytes_accessed=count * triple * 4
        ),
        name="attend",
    )(info, qkv, qkv, qkv, ctx, lse)


def attend_back_kernel(
    info_ref, q_ref, k_ref, v_ref, ctx_ref, lse_ref, dctx_ref, earlier_ref, grad_ref, sum_ref, *, seq
):
    count = q_ref.shape[0]
    lane = lax.broadcasted_iota(jnp.int32, (count, 128), 1)
    bias = key_bias(info_ref[1 + seq], info_ref[0], count)
    scale = HEAD_DIM**-0.5
    query = q_ref[...].astype(f32) * scale
    query_low = query.astype(bf16)
    keys_low = k_ref[...]
    keys = keys_low.astype(f32)
    values = v_ref[...].astype(f32)
    grad_low = dctx_ref[...]
    grad = grad_low.astype(f32)
    product = grad * ctx_ref[...].astype(f32)
    lse_parts = three_parts(-lse_ref[...])
    outs = []
    for head in range(2):
        mine = (lane < 64) if head == 0 else (lane >= 64)
        at = lane - 64 * (1 - head)
        ones = jnp.where((at >= 1) & (at <= 3), 1.0, 0.0)

        def spread(parts, first):
            high, middle, low = parts
            value = jnp.where(at == 2, middle, jnp.where(at == 3, low, 0.0))
            return jnp.where(at == 1, high, jnp.where(at == 0, first, value))

        query_h = jnp.where(mine, query, spread(lse_parts, 1.0)).astype(bf16)
        keys_h = jnp.where(mine, keys, jnp.where(at == 0, bias, ones)).astype(bf16)
        inner = -jnp.sum(jnp.where(mine, product, 0.0), axis=1, keepdims=True)
        inner = jnp.broadcast_to(inner, (count, 128))
        grad_h = jnp.where(mine, grad, spread(three_parts(inner), 0.0)).astype(bf16)
        values_h = jnp.where(mine, values, ones).astype(bf16)
        probs = jnp.exp(dot_nt(keys_h, query_h))
        grad_probs = dot_nt(values_h, grad_h)
        grad_scores = (probs * grad_probs).astype(bf16)
        grad_values = dot(probs.astype(bf16), grad_low)
        grad_keys = dot(grad_scores, query_low)
        grad_query = dot_tn(grad_scores, keys_low) * scale
        outs.append((grad_query, grad_keys, grad_values))
    low = lane < 64
    for c, (first, second) in enumerate(zip(outs[0], outs[1])):
        at = pl.multiple_of((c * pl.num_programs(0) + pl.program_id(0)) * 128, 128)
        both = jnp.where(low, first, second).astype(bf16)
        grad_ref[:, pl.ds(at, 128)] = both
        total = jnp.sum(both.astype(f32), axis=0, keepdims=True)
        sum_ref[:, pl.ds(at, 128)] = jnp.broadcast_to(total, (8, 128))


def attend_back(info, qkv, ctx, lse, grad_ctx, seqs, seq, earlier):
    rows, triple = qkv.shape
    count, pairs = rows // seqs, triple // 3 // 128
    block = lambda at: pl.BlockSpec((count, 128), lambda p, info: (seq, p + at * pairs))
    return pl.pallas_call(
        functools.partial(attend_back_kernel, seq=seq),
        grid_spec=pltpu.PrefetchScalarGridSpec(
            num_scalar_prefetch=1,
            grid=(pairs,),
            in_specs=[block(0), block(1), block(2), block(0), block(0), block(0)]
            + [pl.BlockSpec(memory_space=pl.ANY)],
            out_specs=[
                pl.BlockSpec((count, triple), lambda p, info: (seq, 0)),
                pl.BlockSpec((8, triple), lambda p, info: (0, 0)),
            ],
        ),
        out_shape=[
            jax.ShapeDtypeStruct((rows, triple), bf16),
            jax.ShapeDtypeStruct((8, triple), f32),
        ],
        input_output_aliases={7: 0} if seq else {},
        compiler_params=pltpu.CompilerParams(vmem_limit_bytes=24 << 20),
        cost_estimate=pl.CostEstimate(
            flops=16 * 10**9, transcendentals=count * count * pairs * 2, bytes_accessed=count * triple * 5
        ),
        name="attend_back",
    )(info, qkv, qkv, qkv, ctx, lse, grad_ctx, earlier)


def gelu_and_slope(value):
    size = jnp.abs(value)
    near = 1.0 / (1.0 + (0.3275911 * 0.7071067811865476) * size)
    bell = jnp.exp(-0.5 * (value * value))
    poly = 0.5 * 1.061405429
    poly = poly * near + 0.5 * -1.453152027
    poly = poly * near + 0.5 * 1.421413741
    poly = poly * near + 0.5 * -0.284496736
    poly = poly * near + 0.5 * 0.254829592
    tail = poly * near * bell
    phi = jnp.where(value >= 0, 1.0 - tail, tail)
    return value * phi, phi + value * (bell * 0.3989422804014327)


def up_kernel(h_ref, w_ref, b_ref, _g, _s, g_ref, s_ref):
    rows = h_ref.shape[0]
    step = 256
    for at in range(0, rows, step):
        part = pl.ds(at, step)
        before = dot(h_ref[part, :], w_ref[...]) + b_ref[...]
        hidden, slope = gelu_and_slope(before)
        g_ref[part, :] = hidden.astype(bf16)
        s_ref[part, :] = slope.astype(bf16)


def up(first_low, w_in, b_in, part, hidden, slope):
    rows, width = first_low.shape
    units = w_in.shape[1]
    step = 512
    steps = units // step // 2
    column = lambda size: pl.BlockSpec((size, step), lambda i: (0, i + part * steps))
    return pl.pallas_call(
        up_kernel,
        grid=(steps,),
        in_specs=[pl.BlockSpec((rows, width), lambda i: (0, 0)), column(width), column(1)]
        + [pl.BlockSpec(memory_space=pl.ANY)] * 2,
        out_specs=[column(rows)] * 2,
        out_shape=[jax.ShapeDtypeStruct((rows, units), bf16)] * 2,
        input_output_aliases={3: 0, 4: 1} if part else {},
        compiler_params=pltpu.CompilerParams(vmem_limit_bytes=18 << 20),
        cost_estimate=pl.CostEstimate(
            flops=9 * 10**9, transcendentals=rows * units // 2, bytes_accessed=rows * units * 2
        ),
        name="up",
    )(first_low, w_in, b_in, hidden, slope)


def normalize(values):
    centered = values - jnp.mean(values, axis=-1, keepdims=True)
    inverse = lax.rsqrt(jnp.mean(centered * centered, axis=-1, keepdims=True) + norm_eps)
    return centered * inverse, inverse


def add_sums(ref, lines):
    @pl.when(pl.program_id(0) == 0)
    def _():
        ref[...] = jnp.zeros(ref.shape, f32)

    for i, line in enumerate(lines):
        ref[i : i + 1, :] += jnp.sum(line, axis=0, keepdims=True)


def out_kernel(ctx_ref, w_ref, x_ref, v_ref, first_ref, low_ref, normed_ref, inverse_ref):
    values = x_ref[...].astype(f32) + dot_nt(ctx_ref[...], w_ref[...]) + v_ref[1:2, :]
    normed, inverse = normalize(values)
    first = normed * v_ref[0:1, :] + v_ref[2:3, :]
    first_ref[...] = first
    low_ref[...] = first.astype(bf16)
    normed_ref[...] = normed
    inverse_ref[...] = jnp.broadcast_to(inverse, inverse_ref.shape)


def down_kernel(
    g_ref, w_ref, first_ref, kept_ref, got_ref, v_ref, out_ref, grad_ref, low_ref, sum_ref
):
    values = first_ref[...] + dot_nt(g_ref[...], w_ref[...]) + v_ref[1:2, :]
    normed, inverse = normalize(values)
    out_ref[...] = (normed * v_ref[0:1, :] + v_ref[2:3, :]).astype(bf16)
    mine = pl.program_id(0) % 2 == 0
    given = jnp.where(mine, kept_ref[0].astype(f32), got_ref[0].astype(f32))
    grad = norm_backward(given, normed, inverse, v_ref[0:1, :])
    grad_ref[...] = grad
    low_ref[...] = grad.astype(bf16)
    add_sums(sum_ref, (given * normed, given, grad))


def back_kernel(
    u_ref, w_ref, second_ref, normed_ref, inverse_ref, v_ref, grad_ref, low_ref, sum_ref
):
    given = dot_nt(u_ref[...], w_ref[...]) + second_ref[...]
    normed = normed_ref[...]
    grad = norm_backward(given, normed, inverse_ref[:, :1], v_ref[0:1, :])
    grad_ref[...] = grad
    low_ref[...] = grad.astype(bf16)
    add_sums(sum_ref, (given * normed, given, grad))


def by_rows(kernel, name, rows, step, ins, outs):
    def spec(shape, kind):
        if kind == "rows":
            return pl.BlockSpec((step, shape[1]), lambda i: (i, 0))
        if kind == "half":
            return pl.BlockSpec((1, step, shape[2]), lambda i: (i // 2, 0, 0))
        return pl.BlockSpec(shape, lambda i: (0, 0))

    shapes = [jax.ShapeDtypeStruct(shape, kind) for shape, kind, _ in outs]
    return pl.pallas_call(
        kernel,
        grid=(rows // step,),
        in_specs=[spec(value.shape, kind) for value, kind in ins],
        out_specs=[spec(shape, kind) for shape, _, kind in outs],
        out_shape=shapes,
        compiler_params=pltpu.CompilerParams(vmem_limit_bytes=30 << 20),
        cost_estimate=pl.CostEstimate(
            flops=2 * rows * ins[1][0].size,
            transcendentals=0,
            bytes_accessed=0,
        ),
        name=name,
    )(*[value for value, _ in ins])


def interleave_kernel(own_ref, *refs):
    out_ref, seqs = refs[-1], len(refs) // 2
    is_first = own_ref[0] == 0
    for seq in range(seqs):
        kept, got = refs[2 * seq][...], refs[2 * seq + 1][...].astype(f32)
        out_ref[:, seq, :] = jnp.where(is_first, kept, got)
        out_ref[:, seqs + seq, :] = jnp.where(is_first, got, kept)


def interleave(own, halves):
    count, width = halves[0][0].shape
    step = 64
    block = pl.BlockSpec((step, width), lambda i: (i, 0))
    return pl.pallas_call(
        interleave_kernel,
        grid=(count // step,),
        in_specs=[pl.BlockSpec(memory_space=pltpu.SMEM)] + [block] * (2 * len(halves)),
        out_specs=pl.BlockSpec((step, 2 * len(halves), width), lambda i: (i, 0, 0)),
        out_shape=jax.ShapeDtypeStruct((count, 2 * len(halves), width), f32),
        compiler_params=pltpu.CompilerParams(vmem_limit_bytes=16 << 20),
        name="interleave",
    )(own, *[value for pair in halves for value in pair])


def swap(value, even, odd):
    pairs = [(i, i ^ (odd if i & BIT_CORE else even)) for i in range(PLACES)]
    return lax.ppermute(value, BOTH, pairs)


def slots(me):
    core = (me >> 1) & 1
    for other in (0, 1):
        along = jnp.where((core ^ other) == 0, BIT_X, BIT_Y)
        across = (BIT_X + BIT_Y) - along
        for part, bits in enumerate((0, along, across, BIT_X + BIT_Y)):
            for k in range(4):
                yield other, part, k, me ^ (other * BIT_CORE) ^ bits ^ (k * BIT_Z)


def window(ref, move, place):
    _, rows, _, columns, _, step, start, wide = move
    row = pl.multiple_of((place >> 1 if wide else place) * step, 16)
    if not wide:
        return ref.at[pl.ds(row, rows), :]
    column = pl.multiple_of(start + (place & 1) * columns, 128)
    return ref.at[pl.ds(row, rows), pl.ds(column, columns)]


def place_kernel(me_ref, *refs, moves, outs):
    ins, wholes, sems = refs[:8], refs[8 : 8 + outs], refs[8 + outs]
    for other, part, k, place in slots(me_ref[0]):
        for move in moves:
            row, rows, column, columns, to = move[:5]
            pltpu.make_async_copy(
                ins[4 * other + part].at[k, pl.ds(row, rows), pl.ds(column, columns)],
                window(wholes[to], move, place),
                sems.at[to],
            ).start()
    for to in range(outs):
        pltpu.make_async_copy(wholes[to], wholes[to], sems.at[to]).wait()


def spread_kernel(me_ref, *refs, moves, ins):
    wholes, halves, sems = refs[:ins], refs[ins : ins + 2], refs[ins + 2]
    for other, part, k, place in slots(me_ref[0]):
        for move in moves:
            row, rows, column, columns, to = move[:5]
            pltpu.make_async_copy(
                window(wholes[to], move, place),
                halves[other].at[part, k, pl.ds(row, rows), pl.ds(column, columns)],
                sems.at[other],
            ).start()
    for other in (0, 1):
        pltpu.make_async_copy(halves[other], halves[other], sems.at[other]).wait()


anywhere = pl.BlockSpec(memory_space=pltpu.HBM)
on_core = pl.BlockSpec(memory_space=pltpu.VMEM)


def place(me, parts, moves, shapes):
    return pl.pallas_call(
        functools.partial(place_kernel, moves=moves, outs=len(shapes)),
        in_specs=[pl.BlockSpec(memory_space=pltpu.SMEM)] + [anywhere] * 8,
        out_specs=[on_core] * len(shapes),
        out_shape=[jax.ShapeDtypeStruct(shape, bf16) for shape in shapes],
        compiler_params=pltpu.CompilerParams(vmem_limit_bytes=8 << 20),
        cost_estimate=pl.CostEstimate(
            flops=4 * 10**9, transcendentals=0, bytes_accessed=0
        ),
        scratch_shapes=[pltpu.SemaphoreType.DMA((len(shapes),))],
        name="place",
    )(me, *parts)


def spread(me, wholes, moves, rows, columns):
    return pl.pallas_call(
        functools.partial(spread_kernel, moves=moves, ins=len(wholes)),
        in_specs=[pl.BlockSpec(memory_space=pltpu.SMEM)] + [anywhere] * len(wholes),
        out_specs=[on_core] * 2,
        out_shape=[jax.ShapeDtypeStruct((4, 4, rows, columns), bf16)] * 2,
        compiler_params=pltpu.CompilerParams(vmem_limit_bytes=8 << 20),
        cost_estimate=pl.CostEstimate(
            flops=2 * 10**9, transcendentals=0, bytes_accessed=0
        ),
        scratch_shapes=[pltpu.SemaphoreType.DMA((2,))],
        name="spread",
    )(me, *wholes)


def lines_kernel(v_ref, qkv_ref, one_ref, two_ref, b_ref, *, count, wide):
    places = v_ref.shape[0] // 16
    width = places * count
    qkv_ref[:, width : 2 * width] = jnp.zeros((1, width), f32)
    for place in range(places):
        line = v_ref[pl.ds(place * 16, 16), :].astype(f32)[0:1]
        to = (place % 2) * (places // 2) + place // 2
        qkv_ref[:, to * count : (to + 1) * count] = line[:, :count]
        at = 2 * width + to * count
        qkv_ref[:, at : at + count] = line[:, count : 2 * count]
        b_ref[:, to * wide : (to + 1) * wide] = line[:, 2 * count : 2 * count + wide]
        lines = ((one_ref, 0), (two_ref, 0), (one_ref, 1), (one_ref, 2), (two_ref, 1), (two_ref, 2))
        for i, (ref, at) in enumerate(lines):
            start = 2 * count + wide + i * count
            ref[at : at + 1, to * count : (to + 1) * count] = line[:, start : start + count]


def unpack_lines(vector_rows, count, wide):
    places = vector_rows.shape[0] // 16
    shapes = [(1, 3 * places * count), (3, places * count), (3, places * count), (1, places * wide)]
    return pl.pallas_call(
        functools.partial(lines_kernel, count=count, wide=wide),
        out_shape=[jax.ShapeDtypeStruct(shape, f32) for shape in shapes],
        name="lines",
    )(vector_rows)


def shares_kernel(sums_ref, b_ref, one_ref, two_ref, out_ref, held_ref, *, count, wide, width):
    held_ref[...] = jnp.zeros(held_ref.shape, f32)
    places = held_ref.shape[0] // 16
    for place in range(places):
        at = slice(place * 16, place * 16 + 1)
        to = (place % 2) * (places // 2) + place // 2
        own = slice(to * count, (to + 1) * count)
        last = slice(2 * width + to * count, 2 * width + (to + 1) * count)
        held_ref[at, :count] = sums_ref[0:1, own]
        held_ref[at, count : 2 * count] = sums_ref[0:1, last]
        held_ref[at, 2 * count : 2 * count + wide] = b_ref[:, to * wide : (to + 1) * wide]
        lines = ((one_ref, 0), (two_ref, 0), (one_ref, 2), (one_ref, 1), (two_ref, 2), (two_ref, 1))
        for i, (ref, line) in enumerate(lines):
            start = 2 * count + wide + i * count
            held_ref[at, start : start + count] = ref[line : line + 1, own]
    out_ref[...] = held_ref[...].astype(bf16)


def pack_shares(sums, b_sum, one, two, places, columns, count, wide):
    width = one.shape[1]
    return pl.pallas_call(
        functools.partial(shares_kernel, count=count, wide=wide, width=width),
        out_shape=jax.ShapeDtypeStruct((places * 16, columns), bf16),
        scratch_shapes=[pltpu.VMEM((places * 16, columns), f32)],
        name="shares",
    )(sums, b_sum, one, two)


def move_list(row, blocks, vectors=None):
    moves, at = [], -row
    for to, column, columns, start in blocks:
        at = at if column else at + row
        moves.append((at, row, column, columns, to, row, start, True))
    if vectors:
        moves.append((at + row, 16, 0, blocks[0][2], vectors, 16, 0, False))
    return tuple(moves)


def sync(*values):
    return lax.optimization_barrier(values)


def along_z(shard, direct):
    return [shard] + [swap(shard, BIT_Z * k, BIT_Z * k) for k in (1, 2, 3) if direct]


def far_z(shard, direct):
    return [shard] + [swap(shard, 2 * BIT_Z, 2 * BIT_Z) for _ in (0,) if direct]


def near_z(held, direct):
    if not direct:
        return held
    pair = jnp.stack(held)
    got = swap(pair, BIT_Z, BIT_Z)
    return [pair[0], got[0], pair[1], got[1]]


class Gather:
    def __init__(self, me, group, moves, shapes, direct, early=False):
        self.me, self.moves, self.shapes, self.direct = me, moves, shapes, direct
        self.early = early
        self.held, self.stage = group, 0

    def step(self):
        self.stage += 1
        held = self.held
        if not self.direct:
            return
        if self.stage == 1:
            group = jnp.stack(held)
            self.held = [group, swap(group, BIT_X, BIT_Y), swap(group, BIT_Y, BIT_X)]
            if self.early:
                self.held.append(swap(group, BIT_CORE, BIT_CORE))
        elif self.stage == 2:
            corner = swap(held[1], BIT_Y, BIT_X)
            got = held[3:] + [swap(part, BIT_CORE, BIT_CORE) for part in held[len(held) - 3 : 3]]
            self.held = held[:3] + [corner] + got
        else:
            self.held = held + [swap(held[3], BIT_CORE, BIT_CORE)]

    def whole(self):
        if self.direct:
            return place(self.me, self.held, self.moves, self.shapes)
        everything = lax.all_gather(self.held[0], BOTH, axis=0)
        places = everything.shape[0]
        wholes = []
        for to, shape in enumerate(self.shapes):
            pieces = []
            for row, rows, column, columns, at, _, _, wide in self.moves:
                if at != to:
                    continue
                piece = everything[:, row : row + rows, column : column + columns]
                if wide:
                    piece = piece.reshape(places // 2, 2, rows, columns).transpose(0, 2, 1, 3)
                    pieces.append(piece.reshape(places // 2 * rows, 2 * columns))
                else:
                    pieces.append(piece.reshape(shape))
            wholes.append(jnp.concatenate(pieces, axis=1))
        return wholes


def add_low(*parts):
    return sum(part.astype(f32) for part in parts).astype(bf16)


class Reduce:
    def __init__(self, me, wholes, moves, rows, columns, direct, folded=False):
        self.direct, self.stage, self.folded = direct, 0, folded
        if direct:
            self.held = spread(me, wholes, moves, rows, columns)
            return
        pieces = []
        for _, count, _, wide_columns, to, step, start, wide in moves:
            whole = wholes[to]
            if wide:
                whole = whole[:, start : start + 2 * wide_columns]
                whole = whole.reshape(-1, count, 2, wide_columns).transpose(0, 2, 1, 3)
            pieces.append(whole.reshape(-1, count, wide_columns))
        self.held = [jnp.concatenate(pieces, axis=1)]

    def step(self):
        self.stage += 1
        held = self.held
        if not self.direct:
            return
        if self.stage == 1:
            self.held = [held[0], swap(held[1], BIT_CORE, BIT_CORE)]
        elif self.stage == 2:
            total = [add_low(held[0][at], held[1][at]) for at in range(4)]
            self.held = total[:2] + [swap(total[at], BIT_Y, BIT_X) for at in (2, 3)]
        elif self.stage == 3:
            group, near, far, corner = held
            self.held = [group, far, swap(add_low(near, corner), BIT_X, BIT_Y)]
        elif self.folded and self.stage == 4:
            group = add_low(*held)
            self.held = [group[:2], swap(group[2:], 2 * BIT_Z, 2 * BIT_Z)]
        elif self.folded:
            group = add_low(*held)
            self.held = [group[0], swap(group[1], BIT_Z, BIT_Z)]
        else:
            group = add_low(*held)
            self.held = [group[0]] + [swap(group[k], BIT_Z * k, BIT_Z * k) for k in (1, 2, 3)]

    def shard(self):
        if not self.direct:
            return lax.psum_scatter(self.held[0], BOTH, scatter_dimension=0, tiled=True)[
                0
            ].astype(f32)
        return sum(part.astype(f32) for part in self.held)


def shards(
    tokens, lengths, w_qkv, qkv_bias, w_out, w_in, b_in, w_down, norm_gains, row_biases, cotangent, direct
):
    half_len, seq_count, width = tokens.shape
    own = lax.axis_index("tensor")
    me = (lax.axis_index("dp") * 2 + own).astype(jnp.int32).reshape(1)
    seqs = seq_count // 2
    row = w_qkv.shape[1]
    local_width, local_units = w_qkv.shape[2], w_in.shape[1]
    count = qkv_bias.shape[1]
    units = 2 * local_units
    places = width // row * 2
    total_rows = seqs * 2 * half_len

    def trade(value):
        return lax.ppermute(value, "tensor", [(0, 1), (1, 0)])

    def split_rows(value):
        by_seq = jnp.swapaxes(value, 0, 1)
        kept = lax.dynamic_slice_in_dim(by_seq, own * seqs, seqs, 0)
        return kept, lax.dynamic_slice_in_dim(by_seq, (1 - own) * seqs, seqs, 0)

    def to_rows(value):
        kept, sent = split_rows(value)
        return [kept, trade(sent)]

    def as_rows(halves):
        return jnp.stack(halves, axis=1).reshape(total_rows, width)

    def from_rows(kept, got, kind):
        first = jnp.where(own == 0, kept, got)
        second = jnp.where(own == 0, got, kept)
        return jnp.swapaxes(jnp.concatenate([first, second], axis=0), 0, 1).astype(kind)

    def pack(pieces, kind):
        flat = jnp.concatenate([piece.reshape(piece.shape[0], -1) for piece in pieces], axis=1)
        flat = jnp.pad(flat, ((0, 0), (0, local_width - flat.shape[1])))
        return jnp.pad(flat[:, None, :], ((0, 0), (0, 15), (0, 0))).astype(kind)

    vectors = pack(
        [qkv_bias[None], b_in[None], norm_gains[None], row_biases[None]], bf16
    ).reshape(16, local_width)
    attn_shard = jnp.concatenate([w_qkv.reshape(3 * row, local_width), vectors], axis=0)
    qkv_blocks = [(0, 0, local_width, c * width) for c in range(3)]
    qkv_moves = move_list(row, qkv_blocks, 1)
    upper_moves = move_list(row, [(0, 0, local_units, 0), (1, local_units, local_width, 0)])
    mlp_moves = move_list(row, [(0, 0, local_units, 0)])
    out_moves = move_list(row, [(0, 0, local_width, 0)])
    attn_shapes = [(width, 3 * width), (places * 16, local_width)]

    attn_shard, tokens = sync(attn_shard, tokens)
    attn = Gather(me, along_z(attn_shard, direct), qkv_moves, attn_shapes, direct)
    kept, sent = split_rows(tokens)
    got = [trade(sent[:1])]
    over, under = jnp.concatenate([w_in, w_out.T], axis=1), w_down.T
    attn.held, over, under, kept, got, sent = sync(attn.held, over, under, kept, got, sent)
    attn.step()
    got.append(trade(sent[1:]))
    over = far_z(over, direct)
    under = far_z(under, direct)
    attn.held, over, under, kept, got = sync(attn.held, over, under, kept, got)
    attn.step()
    over = near_z(over, direct)
    rows = as_rows([kept, jnp.concatenate(got, axis=0)])
    attn.held, over, under, rows = sync(attn.held, over, under, rows)
    upper_shapes = [(width, units), (width, width)]
    upper = Gather(me, over, upper_moves, upper_shapes, direct, early=True)
    attn.step()
    under = near_z(under, direct)
    upper.step()
    lower = Gather(me, under, mlp_moves, [(width, units)], direct)
    wq, vector_rows = attn.whole()
    wide = b_in.shape[0]
    if direct:
        qkv_shift, one_lines, two_lines, b_in_all = unpack_lines(vector_rows, count, wide)
    else:
        flat = vector_rows.reshape(places // 2, 2, 16, local_width)[:, :, 0]
        flat = jnp.swapaxes(flat, 0, 1).reshape(places, local_width).astype(f32)

        def vector(at, lines, size):
            piece = flat[:, at : at + lines * size].reshape(places, lines, size)
            return jnp.swapaxes(piece, 0, 1).reshape(lines, places * size)

        bias_pair, b_in_all = vector(0, 2, count), vector(2 * count, 1, wide)
        gains, shifts = vector(2 * count + wide, 2, count), vector(4 * count + wide, 4, count)
        middle = jnp.zeros((width,), f32)
        qkv_shift = jnp.concatenate([bias_pair[0], middle, bias_pair[1]])[None]
        one_lines = jnp.stack([gains[0], shifts[0], shifts[1]])
        two_lines = jnp.stack([gains[1], shifts[2], shifts[3]])

    mine_lengths = lax.dynamic_slice_in_dim(lengths, own * seqs, seqs, 0)
    info = jnp.concatenate([own.reshape(1).astype(jnp.int32), mine_lengths])

    upper.held, wq, qkv_shift = sync(upper.held, wq, qkv_shift)
    upper.step()
    qkv = (dot(rows, wq) + qkv_shift).astype(bf16)
    lower.held, qkv = sync(lower.held, qkv)
    lower.step()
    ctx, lse = attend(info, qkv, seqs, 0, qkv, qkv)
    for seq in range(1, seqs):
        upper.held, ctx, lse = sync(upper.held, ctx, lse)
        if seq == 1:
            upper.step()
        ctx, lse = attend(info, qkv, seqs, seq, ctx, lse)
    upper.held, lower.held, ctx, cotangent = sync(upper.held, lower.held, ctx, cotangent)
    lower.step()
    grad_halves = to_rows(cotangent)
    wi, wo = upper.whole()
    wide_rows = (total_rows, width)
    first, first_low, normed_one, inverse_one = by_rows(
        out_kernel,
        "attention_out",
        total_rows,
        half_len,
        [(ctx, "rows"), (wo, "whole"), (rows, "rows"), (one_lines, "whole")],
        [
            (wide_rows, f32, "rows"),
            (wide_rows, bf16, "rows"),
            (wide_rows, f32, "rows"),
            ((total_rows, 128), f32, "rows"),
        ],
    )
    hidden, slope = up(first_low, wi, b_in_all, 0, first_low, first_low)
    lower.held, hidden, slope = sync(lower.held, hidden, slope)
    lower.step()
    hidden, slope = up(first_low, wi, b_in_all, 1, hidden, slope)
    lower.held, hidden, grad_halves = sync(lower.held, hidden, grad_halves)
    (wd,) = lower.whole()
    output, grad_second, mixed_grad, two_sums = by_rows(
        down_kernel,
        "down",
        total_rows,
        half_len,
        [
            (hidden, "rows"),
            (wd, "whole"),
            (first, "rows"),
            (grad_halves[0], "half"),
            (grad_halves[1], "half"),
            (two_lines, "whole"),
        ],
        [
            (wide_rows, bf16, "rows"),
            (wide_rows, f32, "rows"),
            (wide_rows, bf16, "rows"),
            ((8, width), f32, "whole"),
        ],
    )
    by_half = output.reshape(seqs, 2, half_len, width)
    part_rows = seqs * half_len // 4
    sent_parts = by_half[:, 1].reshape(4, part_rows, width)
    sent_parts, mixed_grad, hidden = sync(
        [sent_parts[i] for i in range(4)], mixed_grad, hidden
    )
    out_parts = [trade(sent_parts[0])]
    grad_wd = dot_tn(mixed_grad, hidden).astype(bf16)
    down = Reduce(me, [grad_wd], mlp_moves, row, local_units, direct, folded=True)
    down.held, mixed_grad, out_parts, sent_parts = sync(
        down.held, mixed_grad, out_parts, sent_parts
    )
    out_parts.append(trade(sent_parts[1]))
    down.step()
    grad_before = (dot(mixed_grad, wd) * slope.astype(f32)).astype(bf16)
    down.held, grad_before, out_parts, sent_parts = sync(
        down.held, grad_before, out_parts, sent_parts
    )
    down.step()
    out_parts.append(trade(sent_parts[2]))
    grad_in_bias = jnp.sum(grad_before, axis=0, dtype=f32)
    grad_wi = dot_tn(first_low, grad_before).astype(bf16)
    into = Reduce(me, [grad_wi], mlp_moves, row, local_units, direct, folded=True)
    into.held, grad_before = sync(into.held, grad_before)
    into.step()
    grad_resid, attn_grad, one_sums = by_rows(
        back_kernel,
        "up_back",
        total_rows,
        half_len,
        [
            (grad_before, "rows"),
            (wi, "whole"),
            (grad_second, "rows"),
            (normed_one, "rows"),
            (inverse_one, "rows"),
            (one_lines, "whole"),
        ],
        [(wide_rows, f32, "rows"), (wide_rows, bf16, "rows"), ((8, width), f32, "whole")],
    )
    grad_wo = dot_tn(attn_grad, ctx).astype(bf16)
    grad_ctx = dot(attn_grad, wo).astype(bf16)
    down.held, into.held, grad_wo, grad_ctx, out_parts = sync(
        down.held, into.held, grad_wo, grad_ctx, out_parts
    )
    down.step()
    into.step()
    outer = Reduce(me, [grad_wo], out_moves, row, local_width, direct, folded=True)
    outer.step()
    count_rows = total_rows // seqs
    grad_triple, sums = attend_back(info, qkv, ctx, lse, grad_ctx, seqs, 0, qkv)
    token_halves = []

    def token_grads(seq):
        mine = slice(seq * count_rows, (seq + 1) * count_rows)
        value = dot_nt(grad_triple[mine], wq) + grad_resid[mine]
        return value[:half_len], value[half_len:].astype(bf16)

    for seq in range(1, seqs):
        first_held = into.held[:3]
        down.held, first_held, outer.held, token_halves, grad_triple = sync(
            down.held, first_held, outer.held, token_halves, grad_triple
        )
        into.held = first_held + into.held[3:]
        if seq == 1:
            down.step()
            outer.step()
        kept, sent = token_grads(seq - 1)
        grad_triple, kept, sent = sync(grad_triple, kept, sent)
        token_halves.append([kept, trade(sent)])
        grad_triple, more = attend_back(info, qkv, ctx, lse, grad_ctx, seqs, seq, grad_triple)
        sums = sums + more
    down.held, into.held, outer.held, token_halves, grad_triple = sync(
        down.held, into.held, outer.held, token_halves, grad_triple
    )
    into.step()
    out_parts.append(trade(sent_parts[3]))
    grad_wq = dot_tn(rows, grad_triple).astype(bf16)

    if direct:
        grad_vectors = pack_shares(
            sums, grad_in_bias[None], one_sums, two_sums, places, local_width, count, wide
        )
    else:

        def shares(value, lines):
            size = value.size // lines // places
            piece = value.reshape(lines, 2, places // 2, size)
            return piece.transpose(2, 1, 0, 3).reshape(places, lines * size)

        grad_pair = jnp.stack([sums[0, :width], sums[0, 2 * width :]])
        one, two = one_sums, two_sums
        grad_lines = [one[0], two[0], one[2], one[1], two[2], two[1]]
        grad_vectors = pack(
            [shares(grad_pair, 2), shares(grad_in_bias, 1), shares(jnp.stack(grad_lines), 6)], bf16
        ).reshape(places * 16, local_width)
    grad_wq, out_parts = sync(grad_wq, out_parts)
    triple = Reduce(
        me, [grad_wq, grad_vectors], qkv_moves, 3 * row + 16, local_width, direct
    )
    triple.held, grad_triple = sync(triple.held, grad_triple)
    triple.step()
    kept, sent = token_grads(seqs - 1)
    triple.held, into.held, kept, sent = sync(triple.held, into.held, kept, sent)
    triple.step()
    into.step()
    down.step()
    outer.step()
    triple.held, down.held, into.held, outer.held, out_parts, by_half, sent = sync(
        triple.held, down.held, into.held, outer.held, out_parts, by_half, sent
    )
    triple.step()
    into.step()
    outer.step()
    out = from_rows(
        by_half[:, 0], jnp.stack(out_parts).reshape(seqs, half_len, width), bf16
    )
    triple.held, into.held, outer.held, sent, out = sync(
        triple.held, into.held, outer.held, sent, out
    )
    triple.step()
    outer.step()
    token_halves.append([kept, trade(sent)])
    d_tokens = interleave(own.reshape(1).astype(jnp.int32), token_halves)
    triple.held, d_tokens = sync(triple.held, d_tokens)
    grad_down = down.shard().T
    grad_in = into.shard()
    grad_out = outer.shard().T
    attn_piece = triple.shard()
    grad_qkv = attn_piece[: 3 * row].reshape(3, row, local_width)
    line = attn_piece[3 * row]

    def cut(at, lines, size):
        return line[at : at + lines * size].reshape(lines, size)

    return (
        out,
        d_tokens,
        grad_qkv,
        cut(0, 2, count),
        grad_out,
        grad_in,
        cut(2 * count, 1, wide)[0],
        grad_down,
        cut(2 * count + wide, 2, count),
        cut(4 * count + wide, 4, count),
    )


def solution(mesh):
    placed = (
        P("tensor", "dp", None),
        P("dp"),
        P(None, "dp", "tensor"),
        P(None, ("tensor", "dp")),
        P("tensor", "dp"),
        P("dp", "tensor"),
        P(("tensor", "dp")),
        P("tensor", "dp"),
        P(None, ("tensor", "dp")),
        P(None, ("tensor", "dp")),
        P("tensor", "dp", None),
    )
    direct = mesh.shape["tensor"] == 2 and mesh.shape["dp"] * 2 == PLACES
    return jax.shard_map(
        functools.partial(shards, direct=direct),
        mesh=mesh,
        in_specs=placed,
        out_specs=(
            P("tensor", "dp", None),
            P("tensor", "dp", None),
            P(None, "dp", "tensor"),
            P(None, ("tensor", "dp")),
            P("tensor", "dp"),
            P("dp", "tensor"),
            P(("tensor", "dp")),
            P("tensor", "dp"),
            P(None, ("tensor", "dp")),
            P(None, ("tensor", "dp")),
        ),
        check_vma=False,
    )
```

```python
import functools

import jax
import jax.numpy as jnp
from jax import lax
from jax.experimental import pallas as pl
from jax.experimental.pallas import tpu as pltpu
from jax.sharding import PartitionSpec as P

HEAD_DIM = 64
BOTH = ("dp", "tensor")
BIT_Y, BIT_CORE, BIT_X, BIT_Z = 1, 2, 4, 8
PLACES = 32

norm_eps = 1e-12
bf16 = jnp.bfloat16
f32 = jnp.float32


def norm_backward(grad, normed, inverse, gain):
    scaled = grad * gain
    inner = (
        scaled
        - jnp.mean(scaled, axis=-1, keepdims=True)
        - normed * jnp.mean(scaled * normed, axis=-1, keepdims=True)
    )
    return inner * inverse


def dot(left, right):
    return jnp.dot(left, right, preferred_element_type=f32)


def dot_nt(left, right):
    return lax.dot_general(left, right, (((1,), (1,)), ((), ())), preferred_element_type=f32)


def dot_tn(left, right):
    return lax.dot_general(left, right, (((0,), (0,)), ((), ())), preferred_element_type=f32)


def three_parts(value):
    high = value.astype(bf16)
    rest = value - high.astype(f32)
    middle = rest.astype(bf16)
    low = (rest - middle.astype(f32)).astype(bf16)
    return high.astype(f32), middle.astype(f32), low.astype(f32)


def key_bias(length, own, count):
    place = lax.broadcasted_iota(jnp.int32, (count, 128), 0)
    place = (place + own * (count // 2)) & (count - 1)
    return jnp.where(place < length, 0.0, -1000000000.0)


def attend_kernel(info_ref, q_ref, k_ref, v_ref, _c, _l, ctx_ref, lse_ref, *, seq):
    count = q_ref.shape[0]
    lane = lax.broadcasted_iota(jnp.int32, (count, 128), 1)
    bias = key_bias(info_ref[1 + seq], info_ref[0], count)
    query = q_ref[...].astype(f32) * (HEAD_DIM**-0.5)
    keys = k_ref[...].astype(f32)
    values = v_ref[...].astype(f32)
    contexts, sums = [], []
    for head in range(2):
        mine = (lane < 64) if head == 0 else (lane >= 64)
        extra = 64 * (1 - head)
        query_h = jnp.where(mine, query, jnp.where(lane == extra, 1.0, 0.0)).astype(bf16)
        keys_h = jnp.where(mine, keys, jnp.where(lane == extra, bias, 0.0)).astype(bf16)
        values_h = jnp.where(mine, values, 1.0).astype(bf16)
        scores = dot_nt(query_h, keys_h)
        peak = jnp.max(scores, axis=1, keepdims=True)
        exponent = jnp.exp(scores - peak).astype(bf16)
        mixed = dot(exponent, values_h)
        total = pltpu.roll(mixed, 64, 1)
        contexts.append(mixed / total)
        sums.append(peak + jnp.log(mixed))
    low = lane < 64
    ctx_ref[...] = jnp.where(low, contexts[0], contexts[1]).astype(bf16)
    lse_ref[...] = jnp.where(low, sums[1], sums[0])


def attend(info, qkv, seqs, seq, ctx, lse):
    rows, triple = qkv.shape
    count, pairs = rows // seqs, triple // 3 // 128
    block = lambda at: pl.BlockSpec((count, 128), lambda p, info: (seq, p + at * pairs))
    return pl.pallas_call(
        functools.partial(attend_kernel, seq=seq),
        grid_spec=pltpu.PrefetchScalarGridSpec(
            num_scalar_prefetch=1,
            grid=(pairs,),
            in_specs=[block(0), block(1), block(2)] + [pl.BlockSpec(memory_space=pl.ANY)] * 2,
            out_specs=[block(0), block(0)],
        ),
        out_shape=[
            jax.ShapeDtypeStruct((rows, triple // 3), bf16),
            jax.ShapeDtypeStruct((rows, triple // 3), f32),
        ],
        input_output_aliases={4: 0, 5: 1} if seq else {},
        compiler_params=pltpu.CompilerParams(vmem_limit_bytes=14 << 20),
        cost_estimate=pl.CostEstimate(
            flops=9 * 10**9, transcendentals=count * count * pairs * 2, bytes_accessed=count * triple * 4
        ),
        name="attend",
    )(info, qkv, qkv, qkv, ctx, lse)


def attend_back_kernel(
    info_ref, q_ref, k_ref, v_ref, ctx_ref, lse_ref, dctx_ref, earlier_ref, grad_ref, sum_ref, *, seq
):
    count = q_ref.shape[0]
    lane = lax.broadcasted_iota(jnp.int32, (count, 128), 1)
    bias = key_bias(info_ref[1 + seq], info_ref[0], count)
    scale = HEAD_DIM**-0.5
    query = q_ref[...].astype(f32) * scale
    query_low = query.astype(bf16)
    keys_low = k_ref[...]
    keys = keys_low.astype(f32)
    values = v_ref[...].astype(f32)
    grad_low = dctx_ref[...]
    grad = grad_low.astype(f32)
    product = grad * ctx_ref[...].astype(f32)
    lse_parts = three_parts(-lse_ref[...])
    outs = []
    for head in range(2):
        mine = (lane < 64) if head == 0 else (lane >= 64)
        at = lane - 64 * (1 - head)
        ones = jnp.where((at >= 1) & (at <= 3), 1.0, 0.0)

        def spread(parts, first):
            high, middle, low = parts
            value = jnp.where(at == 2, middle, jnp.where(at == 3, low, 0.0))
            return jnp.where(at == 1, high, jnp.where(at == 0, first, value))

        query_h = jnp.where(mine, query, spread(lse_parts, 1.0)).astype(bf16)
        keys_h = jnp.where(mine, keys, jnp.where(at == 0, bias, ones)).astype(bf16)
        inner = -jnp.sum(jnp.where(mine, product, 0.0), axis=1, keepdims=True)
        inner = jnp.broadcast_to(inner, (count, 128))
        grad_h = jnp.where(mine, grad, spread(three_parts(inner), 0.0)).astype(bf16)
        values_h = jnp.where(mine, values, ones).astype(bf16)
        probs = jnp.exp(dot_nt(keys_h, query_h))
        grad_probs = dot_nt(values_h, grad_h)
        grad_scores = (probs * grad_probs).astype(bf16)
        grad_values = dot(probs.astype(bf16), grad_low)
        grad_keys = dot(grad_scores, query_low)
        grad_query = dot_tn(grad_scores, keys_low) * scale
        outs.append((grad_query, grad_keys, grad_values))
    low = lane < 64
    for c, (first, second) in enumerate(zip(outs[0], outs[1])):
        at = pl.multiple_of((c * pl.num_programs(0) + pl.program_id(0)) * 128, 128)
        both = jnp.where(low, first, second).astype(bf16)
        grad_ref[:, pl.ds(at, 128)] = both
        total = jnp.sum(both.astype(f32), axis=0, keepdims=True)
        sum_ref[:, pl.ds(at, 128)] = jnp.broadcast_to(total, (8, 128))


def attend_back(info, qkv, ctx, lse, grad_ctx, seqs, seq, earlier):
    rows, triple = qkv.shape
    count, pairs = rows // seqs, triple // 3 // 128
    block = lambda at: pl.BlockSpec((count, 128), lambda p, info: (seq, p + at * pairs))
    return pl.pallas_call(
        functools.partial(attend_back_kernel, seq=seq),
        grid_spec=pltpu.PrefetchScalarGridSpec(
            num_scalar_prefetch=1,
            grid=(pairs,),
            in_specs=[block(0), block(1), block(2), block(0), block(0), block(0)]
            + [pl.BlockSpec(memory_space=pl.ANY)],
            out_specs=[
                pl.BlockSpec((count, triple), lambda p, info: (seq, 0)),
                pl.BlockSpec((8, triple), lambda p, info: (0, 0)),
            ],
        ),
        out_shape=[
            jax.ShapeDtypeStruct((rows, triple), bf16),
            jax.ShapeDtypeStruct((8, triple), f32),
        ],
        input_output_aliases={7: 0} if seq else {},
        compiler_params=pltpu.CompilerParams(vmem_limit_bytes=24 << 20),
        cost_estimate=pl.CostEstimate(
            flops=16 * 10**9, transcendentals=count * count * pairs * 2, bytes_accessed=count * triple * 5
        ),
        name="attend_back",
    )(info, qkv, qkv, qkv, ctx, lse, grad_ctx, earlier)


def gelu_and_slope(value):
    size = jnp.abs(value)
    near = 1.0 / (1.0 + (0.3275911 * 0.7071067811865476) * size)
    bell = jnp.exp(-0.5 * (value * value))
    poly = 0.5 * 1.061405429
    poly = poly * near + 0.5 * -1.453152027
    poly = poly * near + 0.5 * 1.421413741
    poly = poly * near + 0.5 * -0.284496736
    poly = poly * near + 0.5 * 0.254829592
    tail = poly * near * bell
    phi = jnp.where(value >= 0, 1.0 - tail, tail)
    return value * phi, phi + value * (bell * 0.3989422804014327)


def up_kernel(h_ref, w_ref, b_ref, _g, _s, g_ref, s_ref):
    rows = h_ref.shape[0]
    step = 256
    for at in range(0, rows, step):
        part = pl.ds(at, step)
        before = dot(h_ref[part, :], w_ref[...]) + b_ref[...]
        hidden, slope = gelu_and_slope(before)
        g_ref[part, :] = hidden.astype(bf16)
        s_ref[part, :] = slope.astype(bf16)


def up(first_low, w_in, b_in, part, hidden, slope):
    rows, width = first_low.shape
    units = w_in.shape[1]
    step = 512
    steps = units // step // 2
    column = lambda size: pl.BlockSpec((size, step), lambda i: (0, i + part * steps))
    return pl.pallas_call(
        up_kernel,
        grid=(steps,),
        in_specs=[pl.BlockSpec((rows, width), lambda i: (0, 0)), column(width), column(1)]
        + [pl.BlockSpec(memory_space=pl.ANY)] * 2,
        out_specs=[column(rows)] * 2,
        out_shape=[jax.ShapeDtypeStruct((rows, units), bf16)] * 2,
        input_output_aliases={3: 0, 4: 1} if part else {},
        compiler_params=pltpu.CompilerParams(vmem_limit_bytes=18 << 20),
        cost_estimate=pl.CostEstimate(
            flops=9 * 10**9, transcendentals=rows * units // 2, bytes_accessed=rows * units * 2
        ),
        name="up",
    )(first_low, w_in, b_in, hidden, slope)


def normalize(values):
    centered = values - jnp.mean(values, axis=-1, keepdims=True)
    inverse = lax.rsqrt(jnp.mean(centered * centered, axis=-1, keepdims=True) + norm_eps)
    return centered * inverse, inverse


def add_sums(ref, lines):
    @pl.when(pl.program_id(0) == 0)
    def _():
        ref[...] = jnp.zeros(ref.shape, f32)

    for i, line in enumerate(lines):
        ref[i : i + 1, :] += jnp.sum(line, axis=0, keepdims=True)


def out_kernel(ctx_ref, w_ref, x_ref, v_ref, first_ref, low_ref, normed_ref, inverse_ref):
    values = x_ref[...].astype(f32) + dot_nt(ctx_ref[...], w_ref[...]) + v_ref[1:2, :]
    normed, inverse = normalize(values)
    first = normed * v_ref[0:1, :] + v_ref[2:3, :]
    first_ref[...] = first
    low_ref[...] = first.astype(bf16)
    normed_ref[...] = normed
    inverse_ref[...] = jnp.broadcast_to(inverse, inverse_ref.shape)


def down_kernel(
    g_ref, w_ref, first_ref, kept_ref, got_ref, v_ref, out_ref, grad_ref, low_ref, sum_ref
):
    values = first_ref[...] + dot_nt(g_ref[...], w_ref[...]) + v_ref[1:2, :]
    normed, inverse = normalize(values)
    out_ref[...] = (normed * v_ref[0:1, :] + v_ref[2:3, :]).astype(bf16)
    mine = pl.program_id(0) % 2 == 0
    given = jnp.where(mine, kept_ref[0].astype(f32), got_ref[0].astype(f32))
    grad = norm_backward(given, normed, inverse, v_ref[0:1, :])
    grad_ref[...] = grad
    low_ref[...] = grad.astype(bf16)
    add_sums(sum_ref, (given * normed, given, grad))


def back_kernel(
    u_ref, w_ref, second_ref, normed_ref, inverse_ref, v_ref, grad_ref, low_ref, sum_ref
):
    given = dot_nt(u_ref[...], w_ref[...]) + second_ref[...]
    normed = normed_ref[...]
    grad = norm_backward(given, normed, inverse_ref[:, :1], v_ref[0:1, :])
    grad_ref[...] = grad
    low_ref[...] = grad.astype(bf16)
    add_sums(sum_ref, (given * normed, given, grad))


def by_rows(kernel, name, rows, step, ins, outs):
    def spec(shape, kind):
        if kind == "rows":
            return pl.BlockSpec((step, shape[1]), lambda i: (i, 0))
        if kind == "half":
            return pl.BlockSpec((1, step, shape[2]), lambda i: (i // 2, 0, 0))
        return pl.BlockSpec(shape, lambda i: (0, 0))

    shapes = [jax.ShapeDtypeStruct(shape, kind) for shape, kind, _ in outs]
    return pl.pallas_call(
        kernel,
        grid=(rows // step,),
        in_specs=[spec(value.shape, kind) for value, kind in ins],
        out_specs=[spec(shape, kind) for shape, _, kind in outs],
        out_shape=shapes,
        compiler_params=pltpu.CompilerParams(vmem_limit_bytes=30 << 20),
        cost_estimate=pl.CostEstimate(
            flops=2 * rows * ins[1][0].size,
            transcendentals=0,
            bytes_accessed=0,
        ),
        name=name,
    )(*[value for value, _ in ins])


def interleave_kernel(own_ref, *refs):
    out_ref, seqs = refs[-1], len(refs) // 2
    is_first = own_ref[0] == 0
    for seq in range(seqs):
        kept, got = refs[2 * seq][...], refs[2 * seq + 1][...].astype(f32)
        out_ref[:, seq, :] = jnp.where(is_first, kept, got)
        out_ref[:, seqs + seq, :] = jnp.where(is_first, got, kept)


def interleave(own, halves):
    count, width = halves[0][0].shape
    step = 64
    block = pl.BlockSpec((step, width), lambda i: (i, 0))
    return pl.pallas_call(
        interleave_kernel,
        grid=(count // step,),
        in_specs=[pl.BlockSpec(memory_space=pltpu.SMEM)] + [block] * (2 * len(halves)),
        out_specs=pl.BlockSpec((step, 2 * len(halves), width), lambda i: (i, 0, 0)),
        out_shape=jax.ShapeDtypeStruct((count, 2 * len(halves), width), f32),
        compiler_params=pltpu.CompilerParams(vmem_limit_bytes=16 << 20),
        name="interleave",
    )(own, *[value for pair in halves for value in pair])


def swap(value, even, odd):
    pairs = [(i, i ^ (odd if i & BIT_CORE else even)) for i in range(PLACES)]
    return lax.ppermute(value, BOTH, pairs)


def slots(me):
    core = (me >> 1) & 1
    for other in (0, 1):
        along = jnp.where((core ^ other) == 0, BIT_X, BIT_Y)
        across = (BIT_X + BIT_Y) - along
        for part, bits in enumerate((0, along, across, BIT_X + BIT_Y)):
            for k in range(4):
                yield other, part, k, me ^ (other * BIT_CORE) ^ bits ^ (k * BIT_Z)


def window(ref, move, place):
    _, rows, _, columns, _, step, start, wide = move
    row = pl.multiple_of((place >> 1 if wide else place) * step, 16)
    if not wide:
        return ref.at[pl.ds(row, rows), :]
    column = pl.multiple_of(start + (place & 1) * columns, 128)
    return ref.at[pl.ds(row, rows), pl.ds(column, columns)]


def place_kernel(me_ref, *refs, moves, outs):
    ins, wholes, sems = refs[:8], refs[8 : 8 + outs], refs[8 + outs]
    for other, part, k, place in slots(me_ref[0]):
        for move in moves:
            row, rows, column, columns, to = move[:5]
            pltpu.make_async_copy(
                ins[4 * other + part].at[k, pl.ds(row, rows), pl.ds(column, columns)],
                window(wholes[to], move, place),
                sems.at[to],
            ).start()
    for to in range(outs):
        pltpu.make_async_copy(wholes[to], wholes[to], sems.at[to]).wait()


def spread_kernel(me_ref, *refs, moves, ins):
    wholes, halves, sems = refs[:ins], refs[ins : ins + 2], refs[ins + 2]
    for other, part, k, place in slots(me_ref[0]):
        for move in moves:
            row, rows, column, columns, to = move[:5]
            pltpu.make_async_copy(
                window(wholes[to], move, place),
                halves[other].at[part, k, pl.ds(row, rows), pl.ds(column, columns)],
                sems.at[other],
            ).start()
    for other in (0, 1):
        pltpu.make_async_copy(halves[other], halves[other], sems.at[other]).wait()


anywhere = pl.BlockSpec(memory_space=pltpu.HBM)
on_core = pl.BlockSpec(memory_space=pltpu.VMEM)


def place(me, parts, moves, shapes):
    return pl.pallas_call(
        functools.partial(place_kernel, moves=moves, outs=len(shapes)),
        in_specs=[pl.BlockSpec(memory_space=pltpu.SMEM)] + [anywhere] * 8,
        out_specs=[on_core] * len(shapes),
        out_shape=[jax.ShapeDtypeStruct(shape, bf16) for shape in shapes],
        compiler_params=pltpu.CompilerParams(vmem_limit_bytes=8 << 20),
        cost_estimate=pl.CostEstimate(
            flops=4 * 10**9, transcendentals=0, bytes_accessed=0
        ),
        scratch_shapes=[pltpu.SemaphoreType.DMA((len(shapes),))],
        name="place",
    )(me, *parts)


def spread(me, wholes, moves, rows, columns):
    return pl.pallas_call(
        functools.partial(spread_kernel, moves=moves, ins=len(wholes)),
        in_specs=[pl.BlockSpec(memory_space=pltpu.SMEM)] + [anywhere] * len(wholes),
        out_specs=[on_core] * 2,
        out_shape=[jax.ShapeDtypeStruct((4, 4, rows, columns), bf16)] * 2,
        compiler_params=pltpu.CompilerParams(vmem_limit_bytes=8 << 20),
        cost_estimate=pl.CostEstimate(
            flops=2 * 10**9, transcendentals=0, bytes_accessed=0
        ),
        scratch_shapes=[pltpu.SemaphoreType.DMA((2,))],
        name="spread",
    )(me, *wholes)


def lines_kernel(v_ref, qkv_ref, one_ref, two_ref, b_ref, *, count, wide):
    places = v_ref.shape[0] // 16
    width = places * count
    qkv_ref[:, width : 2 * width] = jnp.zeros((1, width), f32)
    for place in range(places):
        line = v_ref[pl.ds(place * 16, 16), :].astype(f32)[0:1]
        to = (place % 2) * (places // 2) + place // 2
        qkv_ref[:, to * count : (to + 1) * count] = line[:, :count]
        at = 2 * width + to * count
        qkv_ref[:, at : at + count] = line[:, count : 2 * count]
        b_ref[:, to * wide : (to + 1) * wide] = line[:, 2 * count : 2 * count + wide]
        lines = ((one_ref, 0), (two_ref, 0), (one_ref, 1), (one_ref, 2), (two_ref, 1), (two_ref, 2))
        for i, (ref, at) in enumerate(lines):
            start = 2 * count + wide + i * count
            ref[at : at + 1, to * count : (to + 1) * count] = line[:, start : start + count]


def unpack_lines(vector_rows, count, wide):
    places = vector_rows.shape[0] // 16
    shapes = [(1, 3 * places * count), (3, places * count), (3, places * count), (1, places * wide)]
    return pl.pallas_call(
        functools.partial(lines_kernel, count=count, wide=wide),
        out_shape=[jax.ShapeDtypeStruct(shape, f32) for shape in shapes],
        name="lines",
    )(vector_rows)


def shares_kernel(sums_ref, b_ref, one_ref, two_ref, out_ref, held_ref, *, count, wide, width):
    held_ref[...] = jnp.zeros(held_ref.shape, f32)
    places = held_ref.shape[0] // 16
    for place in range(places):
        at = slice(place * 16, place * 16 + 1)
        to = (place % 2) * (places // 2) + place // 2
        own = slice(to * count, (to + 1) * count)
        last = slice(2 * width + to * count, 2 * width + (to + 1) * count)
        held_ref[at, :count] = sums_ref[0:1, own]
        held_ref[at, count : 2 * count] = sums_ref[0:1, last]
        held_ref[at, 2 * count : 2 * count + wide] = b_ref[:, to * wide : (to + 1) * wide]
        lines = ((one_ref, 0), (two_ref, 0), (one_ref, 2), (one_ref, 1), (two_ref, 2), (two_ref, 1))
        for i, (ref, line) in enumerate(lines):
            start = 2 * count + wide + i * count
            held_ref[at, start : start + count] = ref[line : line + 1, own]
    out_ref[...] = held_ref[...].astype(bf16)


def pack_shares(sums, b_sum, one, two, places, columns, count, wide):
    width = one.shape[1]
    return pl.pallas_call(
        functools.partial(shares_kernel, count=count, wide=wide, width=width),
        out_shape=jax.ShapeDtypeStruct((places * 16, columns), bf16),
        scratch_shapes=[pltpu.VMEM((places * 16, columns), f32)],
        name="shares",
    )(sums, b_sum, one, two)


def move_list(row, blocks, vectors=None):
    moves, at = [], -row
    for to, column, columns, start in blocks:
        at = at if column else at + row
        moves.append((at, row, column, columns, to, row, start, True))
    if vectors:
        moves.append((at + row, 16, 0, blocks[0][2], vectors, 16, 0, False))
    return tuple(moves)


def sync(*values):
    return lax.optimization_barrier(values)


def along_z(shard, direct):
    return [shard] + [swap(shard, BIT_Z * k, BIT_Z * k) for k in (1, 2, 3) if direct]


def far_z(shard, direct):
    return [shard] + [swap(shard, 2 * BIT_Z, 2 * BIT_Z) for _ in (0,) if direct]


def near_z(held, direct):
    if not direct:
        return held
    pair = jnp.stack(held)
    got = swap(pair, BIT_Z, BIT_Z)
    return [pair[0], got[0], pair[1], got[1]]


class Gather:
    def __init__(self, me, group, moves, shapes, direct, early=False):
        self.me, self.moves, self.shapes, self.direct = me, moves, shapes, direct
        self.early = early
        self.held, self.stage = group, 0

    def step(self):
        self.stage += 1
        held = self.held
        if not self.direct:
            return
        if self.stage == 1:
            group = jnp.stack(held)
            self.held = [group, swap(group, BIT_X, BIT_Y), swap(group, BIT_Y, BIT_X)]
            if self.early:
                self.held.append(swap(group, BIT_CORE, BIT_CORE))
        elif self.stage == 2:
            corner = swap(held[1], BIT_Y, BIT_X)
            got = held[3:] + [swap(part, BIT_CORE, BIT_CORE) for part in held[len(held) - 3 : 3]]
            self.held = held[:3] + [corner] + got
        else:
            self.held = held + [swap(held[3], BIT_CORE, BIT_CORE)]

    def whole(self):
        if self.direct:
            return place(self.me, self.held, self.moves, self.shapes)
        everything = lax.all_gather(self.held[0], BOTH, axis=0)
        places = everything.shape[0]
        wholes = []
        for to, shape in enumerate(self.shapes):
            pieces = []
            for row, rows, column, columns, at, _, _, wide in self.moves:
                if at != to:
                    continue
                piece = everything[:, row : row + rows, column : column + columns]
                if wide:
                    piece = piece.reshape(places // 2, 2, rows, columns).transpose(0, 2, 1, 3)
                    pieces.append(piece.reshape(places // 2 * rows, 2 * columns))
                else:
                    pieces.append(piece.reshape(shape))
            wholes.append(jnp.concatenate(pieces, axis=1))
        return wholes


def add_low(*parts):
    return sum(part.astype(f32) for part in parts).astype(bf16)


class Reduce:
    def __init__(self, me, wholes, moves, rows, columns, direct, folded=False):
        self.direct, self.stage, self.folded = direct, 0, folded
        if direct:
            self.held = spread(me, wholes, moves, rows, columns)
            return
        pieces = []
        for _, count, _, wide_columns, to, step, start, wide in moves:
            whole = wholes[to]
            if wide:
                whole = whole[:, start : start + 2 * wide_columns]
                whole = whole.reshape(-1, count, 2, wide_columns).transpose(0, 2, 1, 3)
            pieces.append(whole.reshape(-1, count, wide_columns))
        self.held = [jnp.concatenate(pieces, axis=1)]

    def step(self):
        self.stage += 1
        held = self.held
        if not self.direct:
            return
        if self.stage == 1:
            self.held = [held[0], swap(held[1], BIT_CORE, BIT_CORE)]
        elif self.stage == 2:
            total = [add_low(held[0][at], held[1][at]) for at in range(4)]
            self.held = total[:2] + [swap(total[at], BIT_Y, BIT_X) for at in (2, 3)]
        elif self.stage == 3:
            group, near, far, corner = held
            self.held = [group, far, swap(add_low(near, corner), BIT_X, BIT_Y)]
        elif self.folded and self.stage == 4:
            group = add_low(*held)
            self.held = [group[:2], swap(group[2:], 2 * BIT_Z, 2 * BIT_Z)]
        elif self.folded:
            group = add_low(*held)
            self.held = [group[0], swap(group[1], BIT_Z, BIT_Z)]
        else:
            group = add_low(*held)
            self.held = [group[0]] + [swap(group[k], BIT_Z * k, BIT_Z * k) for k in (1, 2, 3)]

    def shard(self):
        if not self.direct:
            return lax.psum_scatter(self.held[0], BOTH, scatter_dimension=0, tiled=True)[
                0
            ].astype(f32)
        return sum(part.astype(f32) for part in self.held)


def shards(
    tokens, lengths, w_qkv, qkv_bias, w_out, w_in, b_in, w_down, norm_gains, row_biases, cotangent, direct
):
    half_len, seq_count, width = tokens.shape
    own = lax.axis_index("tensor")
    me = (lax.axis_index("dp") * 2 + own).astype(jnp.int32).reshape(1)
    seqs = seq_count // 2
    row = w_qkv.shape[1]
    local_width, local_units = w_qkv.shape[2], w_in.shape[1]
    count = qkv_bias.shape[1]
    units = 2 * local_units
    places = width // row * 2
    total_rows = seqs * 2 * half_len

    def trade(value):
        return lax.ppermute(value, "tensor", [(0, 1), (1, 0)])

    def split_rows(value):
        by_seq = jnp.swapaxes(value, 0, 1)
        kept = lax.dynamic_slice_in_dim(by_seq, own * seqs, seqs, 0)
        return kept, lax.dynamic_slice_in_dim(by_seq, (1 - own) * seqs, seqs, 0)

    def to_rows(value):
        kept, sent = split_rows(value)
        return [kept, trade(sent)]

    def as_rows(halves):
        return jnp.stack(halves, axis=1).reshape(total_rows, width)

    def from_rows(kept, got, kind):
        first = jnp.where(own == 0, kept, got)
        second = jnp.where(own == 0, got, kept)
        return jnp.swapaxes(jnp.concatenate([first, second], axis=0), 0, 1).astype(kind)

    def pack(pieces, kind):
        flat = jnp.concatenate([piece.reshape(piece.shape[0], -1) for piece in pieces], axis=1)
        flat = jnp.pad(flat, ((0, 0), (0, local_width - flat.shape[1])))
        return jnp.pad(flat[:, None, :], ((0, 0), (0, 15), (0, 0))).astype(kind)

    vectors = pack(
        [qkv_bias[None], b_in[None], norm_gains[None], row_biases[None]], bf16
    ).reshape(16, local_width)
    attn_shard = jnp.concatenate([w_qkv.reshape(3 * row, local_width), vectors], axis=0)
    qkv_blocks = [(0, 0, local_width, c * width) for c in range(3)]
    qkv_moves = move_list(row, qkv_blocks, 1)
    upper_moves = move_list(row, [(0, 0, local_units, 0), (1, local_units, local_width, 0)])
    mlp_moves = move_list(row, [(0, 0, local_units, 0)])
    out_moves = move_list(row, [(0, 0, local_width, 0)])
    attn_shapes = [(width, 3 * width), (places * 16, local_width)]

    attn_shard, tokens = sync(attn_shard, tokens)
    attn = Gather(me, along_z(attn_shard, direct), qkv_moves, attn_shapes, direct)
    kept, sent = split_rows(tokens)
    got = [trade(sent[:1])]
    over, under = jnp.concatenate([w_in, w_out.T], axis=1), w_down.T
    attn.held, over, under, kept, got, sent = sync(attn.held, over, under, kept, got, sent)
    attn.step()
    got.append(trade(sent[1:]))
    over = far_z(over, direct)
    under = far_z(under, direct)
    attn.held, over, under, kept, got = sync(attn.held, over, under, kept, got)
    attn.step()
    over = near_z(over, direct)
    rows = as_rows([kept, jnp.concatenate(got, axis=0)])
    attn.held, over, under, rows = sync(attn.held, over, under, rows)
    upper_shapes = [(width, units), (width, width)]
    upper = Gather(me, over, upper_moves, upper_shapes, direct, early=True)
    attn.step()
    under = near_z(under, direct)
    upper.step()
    lower = Gather(me, under, mlp_moves, [(width, units)], direct)
    wq, vector_rows = attn.whole()
    wide = b_in.shape[0]
    if direct:
        qkv_shift, one_lines, two_lines, b_in_all = unpack_lines(vector_rows, count, wide)
    else:
        flat = vector_rows.reshape(places // 2, 2, 16, local_width)[:, :, 0]
        flat = jnp.swapaxes(flat, 0, 1).reshape(places, local_width).astype(f32)

        def vector(at, lines, size):
            piece = flat[:, at : at + lines * size].reshape(places, lines, size)
            return jnp.swapaxes(piece, 0, 1).reshape(lines, places * size)

        bias_pair, b_in_all = vector(0, 2, count), vector(2 * count, 1, wide)
        gains, shifts = vector(2 * count + wide, 2, count), vector(4 * count + wide, 4, count)
        middle = jnp.zeros((width,), f32)
        qkv_shift = jnp.concatenate([bias_pair[0], middle, bias_pair[1]])[None]
        one_lines = jnp.stack([gains[0], shifts[0], shifts[1]])
        two_lines = jnp.stack([gains[1], shifts[2], shifts[3]])

    mine_lengths = lax.dynamic_slice_in_dim(lengths, own * seqs, seqs, 0)
    info = jnp.concatenate([own.reshape(1).astype(jnp.int32), mine_lengths])

    upper.held, wq, qkv_shift = sync(upper.held, wq, qkv_shift)
    upper.step()
    qkv = (dot(rows, wq) + qkv_shift).astype(bf16)
    lower.held, qkv = sync(lower.held, qkv)
    lower.step()
    ctx, lse = attend(info, qkv, seqs, 0, qkv, qkv)
    for seq in range(1, seqs):
        upper.held, ctx, lse = sync(upper.held, ctx, lse)
        if seq == 1:
            upper.step()
        ctx, lse = attend(info, qkv, seqs, seq, ctx, lse)
    upper.held, lower.held, ctx, cotangent = sync(upper.held, lower.held, ctx, cotangent)
    lower.step()
    grad_halves = to_rows(cotangent)
    wi, wo = upper.whole()
    wide_rows = (total_rows, width)
    first, first_low, normed_one, inverse_one = by_rows(
        out_kernel,
        "attention_out",
        total_rows,
        half_len,
        [(ctx, "rows"), (wo, "whole"), (rows, "rows"), (one_lines, "whole")],
        [
            (wide_rows, f32, "rows"),
            (wide_rows, bf16, "rows"),
            (wide_rows, f32, "rows"),
            ((total_rows, 128), f32, "rows"),
        ],
    )
    hidden, slope = up(first_low, wi, b_in_all, 0, first_low, first_low)
    lower.held, hidden, slope = sync(lower.held, hidden, slope)
    lower.step()
    hidden, slope = up(first_low, wi, b_in_all, 1, hidden, slope)
    lower.held, hidden, grad_halves = sync(lower.held, hidden, grad_halves)
    (wd,) = lower.whole()
    output, grad_second, mixed_grad, two_sums = by_rows(
        down_kernel,
        "down",
        total_rows,
        half_len,
        [
            (hidden, "rows"),
            (wd, "whole"),
            (first, "rows"),
            (grad_halves[0], "half"),
            (grad_halves[1], "half"),
            (two_lines, "whole"),
        ],
        [
            (wide_rows, bf16, "rows"),
            (wide_rows, f32, "rows"),
            (wide_rows, bf16, "rows"),
            ((8, width), f32, "whole"),
        ],
    )
    by_half = output.reshape(seqs, 2, half_len, width)
    part_rows = seqs * half_len // 4
    sent_parts = by_half[:, 1].reshape(4, part_rows, width)
    sent_parts, mixed_grad, hidden = sync(
        [sent_parts[i] for i in range(4)], mixed_grad, hidden
    )
    out_parts = [trade(sent_parts[0])]
    grad_wd = dot_tn(mixed_grad, hidden).astype(bf16)
    down = Reduce(me, [grad_wd], mlp_moves, row, local_units, direct, folded=True)
    down.held, mixed_grad, out_parts, sent_parts = sync(
        down.held, mixed_grad, out_parts, sent_parts
    )
    out_parts.append(trade(sent_parts[1]))
    down.step()
    grad_before = (dot(mixed_grad, wd) * slope.astype(f32)).astype(bf16)
    down.held, grad_before, out_parts, sent_parts = sync(
        down.held, grad_before, out_parts, sent_parts
    )
    down.step()
    out_parts.append(trade(sent_parts[2]))
    grad_in_bias = jnp.sum(grad_before, axis=0, dtype=f32)
    grad_wi = dot_tn(first_low, grad_before).astype(bf16)
    into = Reduce(me, [grad_wi], mlp_moves, row, local_units, direct, folded=True)
    into.held, grad_before = sync(into.held, grad_before)
    into.step()
    grad_resid, attn_grad, one_sums = by_rows(
        back_kernel,
        "up_back",
        total_rows,
        half_len,
        [
            (grad_before, "rows"),
            (wi, "whole"),
            (grad_second, "rows"),
            (normed_one, "rows"),
            (inverse_one, "rows"),
            (one_lines, "whole"),
        ],
        [(wide_rows, f32, "rows"), (wide_rows, bf16, "rows"), ((8, width), f32, "whole")],
    )
    grad_wo = dot_tn(attn_grad, ctx).astype(bf16)
    grad_ctx = dot(attn_grad, wo).astype(bf16)
    down.held, into.held, grad_wo, grad_ctx, out_parts = sync(
        down.held, into.held, grad_wo, grad_ctx, out_parts
    )
    down.step()
    into.step()
    outer = Reduce(me, [grad_wo], out_moves, row, local_width, direct, folded=True)
    outer.step()
    count_rows = total_rows // seqs
    grad_triple, sums = attend_back(info, qkv, ctx, lse, grad_ctx, seqs, 0, qkv)
    token_halves = []

    def token_grads(seq):
        mine = slice(seq * count_rows, (seq + 1) * count_rows)
        value = dot_nt(grad_triple[mine], wq) + grad_resid[mine]
        return value[:half_len], value[half_len:].astype(bf16)

    for seq in range(1, seqs):
        first_held = into.held[:3]
        down.held, first_held, outer.held, token_halves, grad_triple = sync(
            down.held, first_held, outer.held, token_halves, grad_triple
        )
        into.held = first_held + into.held[3:]
        if seq == 1:
            down.step()
            outer.step()
        kept, sent = token_grads(seq - 1)
        grad_triple, kept, sent = sync(grad_triple, kept, sent)
        token_halves.append([kept, trade(sent)])
        grad_triple, more = attend_back(info, qkv, ctx, lse, grad_ctx, seqs, seq, grad_triple)
        sums = sums + more
    down.held, into.held, outer.held, token_halves, grad_triple = sync(
        down.held, into.held, outer.held, token_halves, grad_triple
    )
    into.step()
    out_parts.append(trade(sent_parts[3]))
    grad_wq = dot_tn(rows, grad_triple).astype(bf16)

    if direct:
        grad_vectors = pack_shares(
            sums, grad_in_bias[None], one_sums, two_sums, places, local_width, count, wide
        )
    else:

        def shares(value, lines):
            size = value.size // lines // places
            piece = value.reshape(lines, 2, places // 2, size)
            return piece.transpose(2, 1, 0, 3).reshape(places, lines * size)

        grad_pair = jnp.stack([sums[0, :width], sums[0, 2 * width :]])
        one, two = one_sums, two_sums
        grad_lines = [one[0], two[0], one[2], one[1], two[2], two[1]]
        grad_vectors = pack(
            [shares(grad_pair, 2), shares(grad_in_bias, 1), shares(jnp.stack(grad_lines), 6)], bf16
        ).reshape(places * 16, local_width)
    grad_wq, out_parts, into.held = sync(grad_wq, out_parts, into.held)
    triple = Reduce(
        me, [grad_wq, grad_vectors], qkv_moves, 3 * row + 16, local_width, direct
    )
    triple.held, grad_triple = sync(triple.held, grad_triple)
    triple.step()
    kept, sent = token_grads(seqs - 1)
    triple.held, kept, sent = sync(triple.held, kept, sent)
    triple.step()
    into.step()
    down.step()
    outer.step()
    triple.held, down.held, into.held, outer.held, out_parts, by_half, sent = sync(
        triple.held, down.held, into.held, outer.held, out_parts, by_half, sent
    )
    triple.step()
    into.step()
    outer.step()
    out = from_rows(
        by_half[:, 0], jnp.stack(out_parts).reshape(seqs, half_len, width), bf16
    )
    triple.held, into.held, outer.held, sent, out = sync(
        triple.held, into.held, outer.held, sent, out
    )
    triple.step()
    outer.step()
    token_halves.append([kept, trade(sent)])
    d_tokens = interleave(own.reshape(1).astype(jnp.int32), token_halves)
    triple.held, d_tokens = sync(triple.held, d_tokens)
    grad_down = down.shard().T
    grad_in = into.shard()
    grad_out = outer.shard().T
    attn_piece = triple.shard()
    grad_qkv = attn_piece[: 3 * row].reshape(3, row, local_width)
    line = attn_piece[3 * row]

    def cut(at, lines, size):
        return line[at : at + lines * size].reshape(lines, size)

    return (
        out,
        d_tokens,
        grad_qkv,
        cut(0, 2, count),
        grad_out,
        grad_in,
        cut(2 * count, 1, wide)[0],
        grad_down,
        cut(2 * count + wide, 2, count),
        cut(4 * count + wide, 4, count),
    )


def solution(mesh):
    placed = (
        P("tensor", "dp", None),
        P("dp"),
        P(None, "dp", "tensor"),
        P(None, ("tensor", "dp")),
        P("tensor", "dp"),
        P("dp", "tensor"),
        P(("tensor", "dp")),
        P("tensor", "dp"),
        P(None, ("tensor", "dp")),
        P(None, ("tensor", "dp")),
        P("tensor", "dp", None),
    )
    direct = mesh.shape["tensor"] == 2 and mesh.shape["dp"] * 2 == PLACES
    return jax.shard_map(
        functools.partial(shards, direct=direct),
        mesh=mesh,
        in_specs=placed,
        out_specs=(
            P("tensor", "dp", None),
            P("tensor", "dp", None),
            P(None, "dp", "tensor"),
            P(None, ("tensor", "dp")),
            P("tensor", "dp"),
            P("dp", "tensor"),
            P(("tensor", "dp")),
            P("tensor", "dp"),
            P(None, ("tensor", "dp")),
            P(None, ("tensor", "dp")),
        ),
        check_vma=False,
    )
```
